256 devices in a mesh: blk: 32 (over x_lo, z, core), col: 8 (over y, x_hi).
Axes of the slice: x: 4 (x_hi: 2, x_lo: 2; x = x_hi * 2 + x_lo), y: 4, z: 8, core: 2. Of those that a mesh axis runs over, the one named last changes fastest.
Arguments:
- images: float32 [1152, 16384], P('col', 'blk'), may hold values from -0.8 to 0.8
- texts: float32 [1152, 16384], P('col', 'blk'), may hold values from -0.8 to 0.8
- log_temp: float32 [1], replicated, may hold values from 1.6 to 2.6
- bias: float32 [1], replicated, may hold values from -3 to -1
Outputs:
- loss: float32 [1], replicated
- grad_images: float32 [1152, 16384], P('col', 'blk')
- grad_texts: float32 [1152, 16384], P('col', 'blk')
- grad_log_temp: float32 [1], replicated
- grad_bias: float32 [1], replicated
The draws below stay inside these ranges and needn't reach their ends.
All inputs are finite; a program needn't handle non-finite values.
Results may differ from the reference program's by a relative error of at most 0.00035.
The reference program's roundings to bfloat16 on the way (of `weighted`) count: a program that leaves them out, or rounds other values in their place, can miss the bound.
Values may be sent and summed in bfloat16 or wider, within the bound.
A program may use at most 64 MiB of HBM per device.

```python
import jax
import jax.numpy as jnp
from jax import lax

D = 1152
B = 16384
N_BLK = 32


def levels(stream_key, dims, pieces, smallest, top_value):
    gain = 1.0
    for dim, blocks in pieces:
        draws = jax.random.uniform(jax.random.fold_in(jax.random.fold_in(stream_key, 6), dim), (blocks,), jnp.float32, smallest / len(pieces), top_value / len(pieces))
        gain = gain * jnp.repeat(jnp.exp(draws), dims[dim] // blocks).reshape((-1,) + (1,) * (len(dims) - 1 - dim))
    return gain


def normal_values(rng, dims, scale, most, pieces=(), held_as=jnp.bfloat16):
    array = scale * jax.random.normal(rng, dims, jnp.float32)
    if pieces:
        array = array * levels(rng, dims, pieces, -0.22, 0.18)
    return jnp.clip(array, -most, most).astype(held_as)


def setup_inputs(seed: int = 0) -> dict:
    seeds = jax.random.split(jax.random.key(seed), 5)
    return {
        "images": normal_values(seeds[0], (D, B), 0.1, 0.8, ((0, 8), (1, 32)), jnp.float32),
        "texts": normal_values(seeds[1], (D, B), 0.1, 0.8, ((0, 8), (1, 32)), jnp.float32),
        "log_temp": jnp.clip(jax.random.uniform(seeds[2], (1,), jnp.float32, 1.6, 2.6), 1.6, 2.6),
        "bias": jnp.clip(jax.random.uniform(seeds[3], (1,), jnp.float32, -3.0, -1.0), -3.0, -1.0),
    }


epsilon = 1e-06

def normalize(values):
    scale = lax.rsqrt(lax.optimization_barrier(jnp.sum(values * values, axis=1, keepdims=True)) + epsilon)
    return (values * scale, scale)

def reference(images, texts, log_temp, bias):
    image_rows = images.T
    text_rows = texts.T
    total_rows = image_rows.shape[0]
    width = image_rows.shape[1]
    image_unit, image_scale = normalize(image_rows)
    text_unit, text_scale = normalize(text_rows)
    image_low = image_unit.astype(jnp.bfloat16).astype(jnp.float32)
    text_low = text_unit.astype(jnp.bfloat16).astype(jnp.float32)
    temper = jnp.exp(log_temp[0])
    bias_value = bias[0]
    block_rows = total_rows // N_BLK
    text_blocks = text_low.reshape(N_BLK, block_rows, width)
    image_pos = jnp.arange(total_rows, dtype=jnp.int32)

    def one_block(carried, inputs):
        image_grads, totals = carried
        block_index, text_block = inputs
        scores = jnp.dot(text_block, image_low.T, precision=lax.Precision.HIGHEST)
        text_pos = block_index * block_rows + jnp.arange(block_rows, dtype=jnp.int32)
        labels = jnp.where(text_pos[:, None] == image_pos[None, :], 1.0, -1.0).astype(jnp.float32)
        logits = temper * scores + bias_value
        losses = jax.nn.softplus(-labels * logits)
        slopes = -labels * jax.nn.sigmoid(-labels * logits)
        weighted = (temper * slopes).astype(jnp.bfloat16).astype(jnp.float32)
        image_grads = image_grads + jnp.dot(weighted.T, text_block, precision=lax.Precision.HIGHEST)
        text_grad = jnp.dot(weighted, image_low, precision=lax.Precision.HIGHEST)
        sums = jnp.stack([jnp.sum(losses), jnp.sum(slopes * scores) * temper, jnp.sum(slopes)])
        return ((image_grads, totals + sums), text_grad)
    start = (jnp.zeros((total_rows, width), jnp.float32), jnp.zeros((3,), jnp.float32))
    block_ids = jnp.arange(N_BLK, dtype=jnp.int32)
    (image_grads, totals), text_grads = lax.scan(one_block, start, (block_ids, text_blocks))
    text_grads = text_grads.reshape(total_rows, width)
    grad_images = image_scale * (image_grads - image_unit * lax.optimization_barrier(jnp.sum(image_unit * image_grads, axis=1, keepdims=True)))
    grad_texts = text_scale * (text_grads - text_unit * lax.optimization_barrier(jnp.sum(text_unit * text_grads, axis=1, keepdims=True)))
    pairs = jnp.float32(total_rows) * jnp.float32(total_rows)
    loss = jnp.reshape(totals[0] / pairs, (1,))
    grad_log_temp = jnp.reshape(totals[1] / pairs, (1,))
    grad_bias = jnp.reshape(totals[2] / pairs, (1,))
    return (loss, grad_images.T, grad_texts.T, grad_log_temp, grad_bias)
```

```python
import jax
import jax.numpy as jnp
from jax import lax
from jax.sharding import PartitionSpec as P

epsilon = 1e-06
CONTRACT_ROWS = (((0,), (0,)), ((), ()))
CONTRACT_LANES = (((1,), (1,)), ((), ()))


def per_device(images, texts, log_temp, bias):
    own_index = lax.axis_index("blk")
    col_index = lax.axis_index("col")
    blocks = lax.axis_size("blk")
    cols = lax.axis_size("col")
    pairs_here = images.shape[1]
    both = jnp.stack([images, texts])
    norms = lax.psum(jnp.sum(both * both, axis=1), "col")
    scales = lax.rsqrt(norms + epsilon)[:, None, :]
    units = both * scales
    low = units.astype(jnp.bfloat16)
    image_low = lax.all_gather(low[0], "col", axis=0, tiled=True)
    text_low = lax.all_to_all(low[1], "col", split_axis=1, concat_axis=0, tiled=True)
    text_low = lax.all_gather(text_low, "blk", axis=1, tiled=True)
    temper = jnp.exp(log_temp[0])
    bias_value = bias[0]
    share = pairs_here // cols
    text_count = text_low.shape[1]
    scores = lax.dot_general(text_low, image_low, CONTRACT_ROWS, preferred_element_type=jnp.float32)
    order = jnp.arange(text_count, dtype=jnp.int32)
    text_pos = (order // share) * pairs_here + col_index * share + order % share
    image_pos = own_index * pairs_here + jnp.arange(pairs_here, dtype=jnp.int32)
    labels = jnp.where(text_pos[:, None] == image_pos[None, :], 1.0, -1.0).astype(jnp.float32)
    logits = temper * scores + bias_value
    losses = jax.nn.softplus(-labels * logits)
    slopes = -labels * jax.nn.sigmoid(-labels * logits)
    weighted = (temper * slopes).astype(jnp.bfloat16)
    sums = jnp.stack([jnp.sum(losses), jnp.sum(slopes * scores) * temper, jnp.sum(slopes)])
    image_part = jnp.dot(text_low, weighted, preferred_element_type=jnp.float32)
    text_part = lax.dot_general(image_low, weighted, CONTRACT_LANES, preferred_element_type=jnp.float32)
    image_grad = lax.psum_scatter(image_part, "col", scatter_dimension=0, tiled=True)
    text_grad = lax.psum_scatter(text_part, "blk", scatter_dimension=1, tiled=True)
    text_grad = lax.all_to_all(text_grad, "col", split_axis=0, concat_axis=1, tiled=True)
    grads = jnp.stack([image_grad, text_grad])
    dots = lax.psum(jnp.sum(units * grads, axis=1), "col")[:, None, :]
    grads = scales * (grads - units * dots)
    sums_all = lax.psum(sums, ("blk", "col"))
    total_rows = jnp.float32(pairs_here * blocks)
    pairs = total_rows * total_rows
    loss = jnp.reshape(sums_all[0] / pairs, (1,))
    grad_log_temp = jnp.reshape(sums_all[1] / pairs, (1,))
    grad_bias = jnp.reshape(sums_all[2] / pairs, (1,))
    return (loss, grads[0], grads[1], grad_log_temp, grad_bias)


def solution(mesh):
    in_specs = (P("col", "blk"), P("col", "blk"), P(), P())
    out_specs = (P(), P("col", "blk"), P("col", "blk"), P(), P())
    return jax.shard_map(
        per_device, mesh=mesh, in_specs=in_specs, out_specs=out_specs, check_vma=False
    )
```

```python
import functools

import jax
import jax.numpy as jnp
from jax import lax
from jax.experimental import pallas as pl
from jax.experimental.pallas import tpu as pltpu
from jax.sharding import PartitionSpec as P

epsilon = 1e-06
F32 = jnp.float32
BF16 = jnp.bfloat16
MESH = pl.DeviceIdType.MESH
FEATURES = 1152
SHARE = 144
PAIRS = 512
DMA = pltpu.SemaphoreType.DMA


def device(x, y, z, core):
    return ((x % 2) * 16 + z * 2 + core, y * 2 + x // 2)


def hops(size, way, half):
    return size // 2 if (way == 0) == (half == 0) else size // 2 - 1


def step_of(way):
    return 1 if way == 0 else -1


class Gather:
    def __init__(self, piece, place, size, neighbour, sends, recvs):
        self.piece, self.place, self.size = piece, place, size
        self.neighbour, self.sends, self.recvs = neighbour, sends, recvs

    def copy(self, way, half, t, owner):
        ref = self.piece(owner, half)
        return pltpu.make_async_remote_copy(
            src_ref=ref, dst_ref=ref, send_sem=self.sends.at[way, half, t], recv_sem=self.recvs.at[way, half, t],
            device_id=self.neighbour[way], device_id_type=MESH,
        )

    def chains(self, t):
        return [(w, h) for h in (0, 1) for w in (0, 1) if t < hops(self.size, w, h)]

    def send(self, t):
        for way, half in self.chains(t):
            self.copy(way, half, t, (self.place - step_of(way) * t) % self.size).start()

    def arrive(self, t, then=None):
        for way, half in self.chains(t):
            owner = (self.place - step_of(way) * (t + 1)) % self.size
            self.copy(way, half, t, owner).wait_recv()
            if t + 1 < hops(self.size, way, half):
                self.copy(way, half, t + 1, owner).start()
            if then is not None:
                then(owner, half)

    def finish(self):
        for t in range(self.size // 2):
            for way, half in self.chains(t):
                self.copy(way, half, t, (self.place - step_of(way) * t) % self.size).wait_send()


class Scatter:
    def __init__(self, piece, place, size, neighbour, landed, sends, recvs):
        self.piece, self.place, self.size = piece, place, size
        self.neighbour, self.landed, self.sends, self.recvs = neighbour, landed, sends, recvs

    def copy(self, way, half, t):
        n = hops(self.size, way, half)
        if t == 0:
            src = self.piece((self.place + step_of(way) * n) % self.size, half)
        else:
            src = self.landed.at[way, half, t - 1]
        return pltpu.make_async_remote_copy(
            src_ref=src, dst_ref=self.landed.at[way, half, t], send_sem=self.sends.at[way, half, t],
            recv_sem=self.recvs.at[way, half, t], device_id=self.neighbour[way], device_id_type=MESH,
        )

    def chains(self, t):
        every = [(w, h) for h in (0, 1) for w in (0, 1)]
        every.sort(key=lambda c: -hops(self.size, *c))
        return [c for c in every if t < hops(self.size, *c)]

    def send(self):
        for way, half in self.chains(0):
            self.copy(way, half, 0).start()

    def arrive(self, t):
        for way, half in self.chains(t):
            n = hops(self.size, way, half)
            self.copy(way, half, t).wait_recv()
            own = self.piece((self.place + step_of(way) * (n - t - 1)) % self.size, half)
            slot = self.landed.at[way, half, t]
            if t + 1 < n:
                slot[...] = slot[...] + own[...]
                self.copy(way, half, t + 1).start()
            else:
                own[...] = own[...] + slot[...]

    def finish(self):
        for t in range(self.size // 2):
            for way, half in self.chains(t):
                self.copy(way, half, t).wait_send()


def kernel(
    im_ref, tx_ref, lt_ref, bias_ref,
    loss_ref, gi_ref, gt_ref, glt_ref, gb_ref,
    norm_buf, dot_buf, scale_buf, ts_buf, img, txt, txt_t, wgt, gia, gib, gt, sib_buf,
    land_a1, land_b1, land_a2, land_b2, land_z, sum_buf, tg,
    col_sems, a2a_sems, sib_sems, ga_sems, gb_sems, gz_sems, gy_sems, gx_sems,
    sa_sems, sb_sems, sa2_sems, sb2_sems, sz_sems, total_sems,
):
    b = lax.axis_index("blk")
    c = lax.axis_index("col")
    xlo, z, k = b // 16, (b // 2) % 8, b % 2
    y, xhi = c // 2, c % 2
    x = xhi * 2 + xlo
    fh = 1 - k
    sibling = device(x, y, z, 1 - k)
    x_near = [device((x + 1) % 4, y, z, k), device((x + 3) % 4, y, z, k)]
    y_near = [device(x, (y + 1) % 4, z, k), device(x, (y + 3) % 4, z, k)]
    z_near = [device(x, y, (z + 1) % 8, k), device(x, y, (z + 7) % 8, k)]
    x_other = device(xhi * 2 + 1 - xlo, y, z, k)
    col_peers = [(b, (c + i) % 8) for i in range(1, 8)]
    z_peers = [device(x, y, (z + i) % 8, k) for i in range(1, 8)]
    text_to = [(xlo * 16 + z * 2 + 1 - c // 4, 4 * k + s) for s in range(4)]
    text_from = [(xlo * 16 + z * 2 + c // 4, 4 * fh + i) for i in range(4)]

    barrier = pltpu.get_barrier_semaphore()
    greeted = [sibling] + x_near + col_peers + z_peers + text_to + text_from
    for peer in greeted:
        pl.semaphore_signal(barrier, inc=1, device_id=peer, device_id_type=MESH)

    def remote(src, dst, send_sem, recv_sem, peer):
        return pltpu.make_async_remote_copy(
            src_ref=src, dst_ref=dst, send_sem=send_sem, recv_sem=recv_sem, device_id=peer, device_id_type=MESH
        )

    im = im_ref[...]
    tx = tx_ref[...]
    norm_buf[c, 0:1, :] = jnp.sum(im * im, axis=0, keepdims=True)
    norm_buf[c, 1:2, :] = jnp.sum(tx * tx, axis=0, keepdims=True)
    pl.semaphore_wait(barrier, len(greeted))

    def over_col(buf, stage):
        def copies():
            return [
                remote(buf.at[c], buf.at[c], col_sems.at[stage, 0, i], col_sems.at[stage, 1, i], col_peers[i])
                for i in range(7)
            ]

        for copy in copies():
            copy.start()
        for i in range(7):
            src = buf.at[(c + 7 - i) % 8]
            remote(src, src, col_sems.at[stage, 0, i], col_sems.at[stage, 1, i], col_peers[i]).wait_recv()
        return copies

    norms_out = over_col(norm_buf, 0)
    norms = norm_buf[0]
    for i in range(1, 8):
        norms = norms + norm_buf[i]
    scale_buf[...] = lax.rsqrt(norms + epsilon)
    scale_i = scale_buf[0:1, :]
    scale_t = scale_buf[1:2, :]

    ts_buf[...] = (tx_ref[...] * scale_t).astype(BF16)
    own_cols = pl.ds(pl.multiple_of(z * 128, 128), 128)
    text_sends = []
    for s in range(4):
        copy = remote(
            ts_buf.at[:, pl.ds(s * 128, 128)],
            txt.at[pl.ds(pl.multiple_of(c * SHARE, 16), SHARE), own_cols],
            a2a_sems.at[0, 0, s], a2a_sems.at[0, 1, c % 4], text_to[s],
        )
        copy.start()
        text_sends.append(copy)
    im_low = (im_ref[...] * scale_i).astype(BF16)
    im_rows = pl.ds(pl.multiple_of(xhi * SHARE, 16), SHARE)
    im_cols = pl.ds(pl.multiple_of(xlo * 256, 256), 256)
    img[0, y, im_rows, im_cols] = im_low[:, 0:256]
    img[1, y, im_rows, im_cols] = im_low[:, 256:512]

    def rows_of(xx):
        return pl.ds(pl.multiple_of((xx // 2) * SHARE, 16), SHARE)

    def near_cols(xx, half):
        return pl.ds(pl.multiple_of((xx % 2) * 256 + half * 128, 128), 128)

    ga = Gather(lambda o, h: img.at[0, y, rows_of(o), near_cols(o, h)], x, 4, x_near, ga_sems.at[0], ga_sems.at[1])
    gb = Gather(lambda o, h: img.at[1, o, im_rows, near_cols(x, h)], y, 4, y_near, gb_sems.at[0], gb_sems.at[1])
    gy = Gather(lambda o, h: img.at[0, o, pl.ds(h * SHARE, SHARE), :], y, 4, y_near, gy_sems.at[0], gy_sems.at[1])
    gx = Gather(
        lambda o, h: img.at[1, pl.ds(h * 2, 2), rows_of(o), pl.ds(pl.multiple_of((o % 2) * 256, 256), 256)],
        x, 4, x_near, gx_sems.at[0], gx_sems.at[1],
    )

    def text_piece(o, h):
        return txt.at[pl.ds(pl.multiple_of(fh * 576 + h * 288, 16), 288), pl.ds(pl.multiple_of(o * 128, 128), 128)]

    gz = Gather(text_piece, z, 8, z_near, gz_sems.at[0], gz_sems.at[1])

    def to_sibling(o, h):
        ref = text_piece(o, h)
        remote(ref, ref, sib_sems.at[0], sib_sems.at[1], sibling).start()

    ga.send(0)
    gb.send(0)
    for i in range(4):
        ref = txt.at[pl.ds(pl.multiple_of(fh * 576 + i * SHARE, 16), SHARE), own_cols]
        remote(ref, ref, a2a_sems.at[0, 0, i], a2a_sems.at[0, 1, i], sibling).wait_recv()
    gz.send(0)
    to_sibling(z, 0)
    to_sibling(z, 1)
    ga.arrive(0)
    gb.arrive(0)
    ga.arrive(1)
    gy.send(0)
    gb.arrive(1)
    gx.send(0)
    gz.arrive(0, to_sibling)
    gz.arrive(1, to_sibling)
    gy.arrive(0)
    gx.arrive(0)
    gz.arrive(2, to_sibling)
    gz.arrive(3, to_sibling)
    theirs = txt.at[pl.ds(pl.multiple_of((1 - fh) * 576, 16), 576), :]
    mine = txt.at[pl.ds(pl.multiple_of(fh * 576, 16), 576), :]
    remote(mine, theirs, sib_sems.at[0], sib_sems.at[1], sibling).wait_recv()

    def turn(o, _):
        cols = pl.ds(pl.multiple_of(o * 128, 128), 128)
        txt_t[cols, :] = txt[:, cols].T
        return 0

    lax.fori_loop(0, 8, turn, 0)
    gy.arrive(1)
    gx.arrive(1)

    temper = jnp.exp(jnp.full((1, 256), lt_ref[0], F32))
    bias_value = bias_ref[0]
    sum_buf[0] = jnp.zeros((3, 8, 128), F32)

    def tile(i, _):
        h, n, m = i // 4, (i // 2) % 2, i % 2
        rows = pl.ds(pl.multiple_of(m * 512, 512), 512)
        cols = pl.ds(pl.multiple_of(n * 256, 256), 256)
        images = img[h, :, :, cols].reshape(FEATURES, 256)
        scores = jnp.dot(txt_t[rows, :], images, preferred_element_type=F32)
        j = lax.broadcasted_iota(jnp.int32, (512, 1), 0) + m * 512
        text_pos = (xlo * 16 + (j // 128) * 2 + c // 4) * PAIRS + (c % 4) * 128 + j % 128
        image_pos = (n * 16 + z * 2 + k) * PAIRS + h * 256 + lax.broadcasted_iota(jnp.int32, (1, 256), 1)
        same = text_pos == image_pos
        logits = temper * scores + bias_value
        u = jnp.where(same, -logits, logits)
        e = jnp.exp(-jnp.abs(u))
        r = 1.0 / (1.0 + e)
        sig = jnp.where(u >= 0, r, e * r)
        losses = jnp.maximum(u, 0.0) + jnp.log1p(e)
        slopes = jnp.where(same, -sig, sig)
        wgt[h, rows, cols] = (temper * slopes).astype(BF16)

        def fold(v):
            v = jnp.sum(v.reshape(64, 8, 256), axis=0)
            return v[:, 0:128] + v[:, 128:256]

        sum_buf[0, 0] += fold(losses)
        sum_buf[0, 1] += fold(slopes * scores)
        sum_buf[0, 2] += fold(slopes)
        return 0

    lax.fori_loop(0, 8, tile, 0)

    def total_stage(stage, base, peers, sources):
        copies = []
        for i, peer in enumerate(peers):
            copies.append(remote(
                sum_buf.at[base], sum_buf.at[base + 1 + i],
                total_sems.at[0, stage, i], total_sems.at[1, stage, i], peer,
            ))
        for copy in copies:
            copy.start()

        def done():
            for copy in copies:
                copy.wait()
            total = sum_buf[base]
            for i in range(len(peers)):
                total = total + sum_buf[base + 1 + i]
            sum_buf[base + 1 + len(peers)] = total

        return done

    s_sib = total_stage(0, 0, [sibling], None)

    def text_part(n, _):
        rows = pl.ds(pl.multiple_of(n * 256, 256), 256)
        contract = (((1,), (1,)), ((), ()))
        part = lax.dot_general(
            img[0].reshape(FEATURES, 512), wgt[0, rows, :], contract, preferred_element_type=F32
        ) + lax.dot_general(img[1].reshape(FEATURES, 512), wgt[1, rows, :], contract, preferred_element_type=F32)
        gt[2 * n] = part[:, 0:128]
        gt[2 * n + 1] = part[:, 128:256]
        return 0

    lax.fori_loop(0, 4, text_part, 0)
    grad_sib = remote(
        gt.at[:, pl.ds(pl.multiple_of((1 - fh) * 576, 8), 576), :], sib_buf, sib_sems.at[2], sib_sems.at[3], sibling
    )
    grad_sib.start()
    s_sib()
    s_x = total_stage(1, 2, [x_other], None)

    def image_part(h):
        def body(n, _):
            cols = pl.ds(pl.multiple_of(n * 256, 256), 256)
            part = jnp.dot(txt[...], wgt[h, :, cols], preferred_element_type=F32)
            for yy in range(4):
                for hi in range(2):
                    piece = part[yy * 288 + hi * SHARE : yy * 288 + hi * SHARE + SHARE, :]
                    if h == 0:
                        gia[yy, hi * 2 + n] = piece
                    else:
                        gib[hi * 2 + n, yy] = piece
            return 0

        lax.fori_loop(0, 2, body, 0)

    pair = lambda h: pl.ds(h * 2, 2)
    near = lambda h: pl.ds(h * 72, 72)
    sa = Scatter(lambda o, h: gia.at[o, pair(h)], y, 4, y_near, land_a1, sa_sems.at[0], sa_sems.at[1])
    sb = Scatter(lambda o, h: gib.at[o, pair(h)], x, 4, x_near, land_b1, sb_sems.at[0], sb_sems.at[1])
    sa2 = Scatter(lambda o, h: gia.at[y, o, near(h)], x, 4, x_near, land_a2, sa2_sems.at[0], sa2_sems.at[1])
    sb2 = Scatter(lambda o, h: gib.at[x, o, near(h)], y, 4, y_near, land_b2, sb2_sems.at[0], sb2_sems.at[1])
    gt_rows = lambda h: pl.ds(pl.multiple_of(fh * 576 + h * 288, 8), 288)
    sz = Scatter(lambda o, h: gt.at[o, gt_rows(h)], z, 8, z_near, land_z, sz_sems.at[0], sz_sems.at[1])

    image_part(0)
    sa.send()
    s_x()
    s_z = total_stage(2, 4, z_peers, None)
    grad_sib.wait()
    own_half = pl.ds(pl.multiple_of(fh * 576, 8), 576)

    def join(o, _):
        gt[o, own_half] = gt[o, own_half] + sib_buf[o]
        return 0

    lax.fori_loop(0, 8, join, 0)
    sz.send()
    image_part(1)
    sb.send()
    s_z()
    s_col = total_stage(3, 12, col_peers, None)
    sz.arrive(0)
    s_col()
    total = sum_buf[20]
    pairs_inv = 1.0 / float(16384 * 16384)
    loss_ref[0] = jnp.sum(total[0]) * pairs_inv
    glt_ref[0] = jnp.sum(total[1] * temper[:, 0:128]) * pairs_inv
    gb_ref[0] = jnp.sum(total[2]) * pairs_inv
    sz.arrive(1)
    sa.arrive(0)
    sb.arrive(0)
    sz.arrive(2)
    sa.arrive(1)
    sa2.send()
    sb.arrive(1)
    sb2.send()
    sz.arrive(3)

    back = []
    for i in range(4):
        copy = remote(
            gt.at[z, pl.ds(pl.multiple_of(fh * 576 + i * SHARE, 8), SHARE), :],
            tg.at[:, pl.ds(pl.multiple_of((c % 4) * 128, 128), 128)],
            a2a_sems.at[1, 0, i], a2a_sems.at[1, 1, c % 4], text_from[i],
        )
        copy.start()
        back.append(copy)
    sa2.arrive(0)
    sb2.arrive(0)
    sa2.arrive(1)
    sb2.arrive(1)
    grad_a = gia[y, x]
    grad_b = gib[x, y]
    unit_i = im_ref[...] * scale_buf[0:1, :]
    dot_buf[c, 0:1, 0:256] = jnp.sum(unit_i[:, 0:256] * grad_a, axis=0, keepdims=True)
    dot_buf[c, 0:1, 256:512] = jnp.sum(unit_i[:, 256:512] * grad_b, axis=0, keepdims=True)
    for s in range(4):
        ref = tg.at[:, pl.ds(s * 128, 128)]
        remote(ref, ref, a2a_sems.at[1, 0, s], a2a_sems.at[1, 1, s], sibling).wait_recv()
    unit_t = tx_ref[...] * scale_buf[1:2, :]
    dot_buf[c, 1:2, :] = jnp.sum(unit_t * tg[...], axis=0, keepdims=True)
    dots_out = over_col(dot_buf, 1)
    dots = dot_buf[0]
    for i in range(1, 8):
        dots = dots + dot_buf[i]
    scale_i = scale_buf[0:1, :]
    scale_t = scale_buf[1:2, :]
    unit_i = im_ref[...] * scale_i
    unit_t = tx_ref[...] * scale_t
    gi_ref[:, 0:256] = scale_i[:, 0:256] * (gia[y, x] - unit_i[:, 0:256] * dots[0:1, 0:256])
    gi_ref[:, 256:512] = scale_i[:, 256:512] * (gib[x, y] - unit_i[:, 256:512] * dots[0:1, 256:512])
    gt_ref[...] = scale_t * (tg[...] - unit_t * dots[1:2, :])

    for copies in (norms_out, dots_out):
        for copy in copies():
            copy.wait_send()
    for copy in text_sends + back:
        copy.wait_send()
    remote(mine, theirs, sib_sems.at[0], sib_sems.at[1], sibling).wait_send()
    for stage in (ga, gb, gy, gx, gz, sa, sb, sa2, sb2, sz):
        stage.finish()


def per_device(images, texts, log_temp, bias):
    vmem = pl.BlockSpec(memory_space=pltpu.VMEM)
    smem = pl.BlockSpec(memory_space=pltpu.SMEM)
    one = jax.ShapeDtypeStruct((1,), F32)
    grad = jax.ShapeDtypeStruct((SHARE, PAIRS), F32)
    scratch = [
        pltpu.VMEM((8, 8, PAIRS), F32),
        pltpu.VMEM((8, 8, PAIRS), F32),
        pltpu.VMEM((8, PAIRS), F32),
        pltpu.VMEM((SHARE, PAIRS), BF16),
        pltpu.VMEM((2, 4, 2 * SHARE, 512), BF16),
        pltpu.VMEM((FEATURES, 1024), BF16),
        pltpu.VMEM((1024, FEATURES), BF16),
        pltpu.VMEM((2, 1024, 512), BF16),
        pltpu.VMEM((4, 4, SHARE, 256), F32),
        pltpu.VMEM((4, 4, SHARE, 256), F32),
        pltpu.VMEM((8, FEATURES, 128), F32),
        pltpu.VMEM((8, 576, 128), F32),
        pltpu.VMEM((2, 2, 2, 2, SHARE, 256), F32),
        pltpu.VMEM((2, 2, 2, 2, SHARE, 256), F32),
        pltpu.VMEM((2, 2, 2, 72, 256), F32),
        pltpu.VMEM((2, 2, 2, 72, 256), F32),
        pltpu.VMEM((2, 2, 4, 288, 128), F32),
        pltpu.VMEM((21, 3, 8, 128), F32),
        pltpu.VMEM((SHARE, PAIRS), F32),
        DMA((2, 2, 7)),
        DMA((2, 2, 4)),
        DMA((4,)),
        DMA((2, 2, 2, 2)), DMA((2, 2, 2, 2)),
        DMA((2, 2, 2, 4)),
        DMA((2, 2, 2, 2)), DMA((2, 2, 2, 2)),
        DMA((2, 2, 2, 2)), DMA((2, 2, 2, 2)), DMA((2, 2, 2, 2)), DMA((2, 2, 2, 2)),
        DMA((2, 2, 2, 4)),
        DMA((2, 4, 7)),
    ]
    return pl.pallas_call(
        kernel,
        out_shape=(one, grad, grad, one, one),
        in_specs=[vmem, vmem, smem, smem],
        out_specs=(smem, vmem, vmem, smem, smem),
        scratch_shapes=scratch,
        compiler_params=pltpu.CompilerParams(
            collective_id=0, has_side_effects=True, vmem_limit_bytes=56 * 2**20
        ),
        name="contrastive",
    )(images, texts, log_temp, bias)


def solution(mesh):
    in_specs = (P("col", "blk"), P("col", "blk"), P(), P())
    out_specs = (P(), P("col", "blk"), P("col", "blk"), P(), P())
    return jax.shard_map(
        per_device, mesh=mesh, in_specs=in_specs, out_specs=out_specs, check_vma=False
    )
```

```python
import functools

import jax
import jax.numpy as jnp
from jax import lax
from jax.experimental import pallas as pl
from jax.experimental.pallas import tpu as pltpu
from jax.sharding import PartitionSpec as P

epsilon = 1e-06
F32 = jnp.float32
BF16 = jnp.bfloat16
MESH = pl.DeviceIdType.MESH
FEATURES = 1152
NT = (((1,), (1,)), ((), ()))
SHARE = 144
PAIRS = 512
DMA = pltpu.SemaphoreType.DMA


def device(x, y, z, core):
    return ((x % 2) * 16 + z * 2 + core, y * 2 + x // 2)


class Ring:
    def __init__(self, piece, place, size, neighbour, chains, sends, recvs, landed=None):
        self.piece, self.place, self.size, self.neighbour = piece, place, size, neighbour
        self.sends, self.recvs, self.landed = sends, recvs, landed
        self.all = []
        base = 0
        for way, half, n in chains:
            self.all.append((way, half, n, base))
            base += n

    def at(self, offset):
        return (self.place + offset + 2 * self.size) % self.size

    def chains(self, t):
        return [chain for chain in self.all if t < chain[2]]

    def remote(self, chain, t, src, dst):
        way, _, _, base = chain
        return pltpu.make_async_remote_copy(
            src_ref=src, dst_ref=dst, send_sem=self.sends.at[base + t], recv_sem=self.recvs.at[base + t],
            device_id=self.neighbour[way], device_id_type=MESH,
        )

    def send(self, only=None):
        for chain in self.all:
            if only is None or chain[:2] in only:
                self.copy(chain, 0).start()

    def finish(self):
        for t in range(self.size):
            for chain in self.chains(t):
                self.copy(chain, t).wait_send()


class Gather(Ring):
    def copy(self, chain, t):
        way, half = chain[:2]
        ref = self.piece(self.at(-t if way == 0 else t), half)
        return self.remote(chain, t, ref, ref)

    def arrive(self, t, then=None, only=None):
        for chain in self.chains(t):
            way, half, n, base = chain
            if only is not None and chain[:2] not in only:
                continue
            owner = self.at(-t - 1 if way == 0 else t + 1)
            ref = self.piece(owner, half)
            self.remote(chain, t, ref, ref).wait_recv()
            if t + 1 < n:
                self.copy(chain, t + 1).start()
            if then is not None:
                then(owner, half, base + t)


class Scatter(Ring):
    def copy(self, chain, t):
        way, half, n, base = chain
        if t == 0:
            src = self.piece(self.at(n if way == 0 else -n), half)
        else:
            src = self.landed.at[base + t - 1]
        return self.remote(chain, t, src, self.landed.at[base + t])

    def arrive(self, t, only=None):
        for chain in self.chains(t):
            way, half, n, base = chain
            if only is not None and chain[:2] not in only:
                continue
            self.copy(chain, t).wait_recv()
            ahead = n - t - 1
            own = self.piece(self.at(ahead if way == 0 else -ahead), half)
            slot = self.landed.at[base + t]
            if ahead > 0:
                slot[...] = slot[...] + own[...]
                self.copy(chain, t + 1).start()
            else:
                own[...] = own[...] + slot[...]


class Direct:
    def __init__(self, piece, place, axis, sends, recvs, landed=None):
        self.piece, self.place, self.axis = piece, place, axis
        self.sends, self.recvs, self.landed = sends, recvs, landed

    def copy(self, i):
        if self.landed is None:
            src = dst = self.piece(self.place, 0)
        else:
            src, dst = self.piece((self.place + i + 1) % 4, 0), self.landed.at[i]
        return pltpu.make_async_remote_copy(
            src_ref=src, dst_ref=dst, send_sem=self.sends.at[i], recv_sem=self.recvs.at[i],
            device_id=self.axis(i + 1), device_id_type=MESH,
        )

    def send(self):
        for i in (1, 0, 2):
            self.copy(i).start()

    def arrive(self):
        for i in range(3):
            self.copy(i).wait_recv()
        if self.landed is not None:
            own = self.piece(self.place, 0)
            own[...] = own[...] + (self.landed[0] + self.landed[1] + self.landed[2])

    def finish(self):
        for i in range(3):
            self.copy(i).wait_send()


def finish_all(started):
    for finish in started:
        finish()


def kernel(
    im_ref, tx_ref, knob_ref,
    mean_ref, gi_ref, gt_ref,
    norm_buf, dot_buf, scale_buf, ts_buf, img, txt, txt_t, wgt, gi, gt, sib_buf,
    land_1, land_2, land_z, sum_buf, sum_z, tg,
    col_sems, a2a_sems, sib_sems, pair_sems, g_sems, gz_sems, s_sems, sz_sems, gs_sems, total_sems,
):
    b = lax.axis_index("blk")
    c = lax.axis_index("col")
    xlo, z, k = b // 16, (b // 2) % 8, b % 2
    y, xhi = c // 2, c % 2
    x = xhi * 2 + xlo
    fh = 1 - k
    sibling = device(x, y, z, 1 - k)
    x_near = [device((x + 1) % 4, y, z, k), device((x + 3) % 4, y, z, k)]
    y_near = [device(x, (y + 1) % 4, z, k), device(x, (y + 3) % 4, z, k)]
    on_x = lambda i: device((x + i) % 4, y, z, k)
    on_y = lambda i: device(x, (y + i) % 4, z, k)
    z_near = [device(x, y, (z + 1) % 8, k), device(x, y, (z + 7) % 8, k)]
    x_other = device(xhi * 2 + 1 - xlo, y, z, k)
    col_peers = [(b, (c + i) % 8) for i in range(1, 8)]
    across = [(xlo * 16 + z * 2 + 1 - k, 4 * (c // 4) + i) for i in range(4)]
    text_to = [(xlo * 16 + z * 2 + 1 - c // 4, 4 * k + s) for s in range(4)]
    text_from = [(xlo * 16 + z * 2 + c // 4, 4 * fh + i) for i in range(4)]
    started = []

    barrier = pltpu.get_barrier_semaphore()
    greeted = across + x_near + z_near + col_peers
    for peer in greeted:
        pl.semaphore_signal(barrier, inc=1, device_id=peer, device_id_type=MESH)

    def remote(src, dst, send_sem, recv_sem, peer):
        return pltpu.make_async_remote_copy(
            src_ref=src, dst_ref=dst, send_sem=send_sem, recv_sem=recv_sem, device_id=peer, device_id_type=MESH
        )

    im = im_ref[...]
    tx = tx_ref[...]
    norm_buf[c, 0:1, :] = jnp.sum(im * im, axis=0, keepdims=True)
    norm_buf[c, 1:2, :] = jnp.sum(tx * tx, axis=0, keepdims=True)
    pl.semaphore_wait(barrier, len(greeted))

    def over_col(buf, stage):
        sends = [
            remote(buf.at[c], buf.at[c], col_sems.at[stage, 0, i], col_sems.at[stage, 1, i], col_peers[i])
            for i in range(7)
        ]
        for copy in sends:
            copy.start()
        started.append(lambda: [copy.wait_send() for copy in sends])

        def total():
            for i in range(7):
                src = buf.at[(c + 7 - i) % 8]
                remote(src, src, col_sems.at[stage, 0, i], col_sems.at[stage, 1, i], col_peers[i]).wait_recv()
            whole = buf[0]
            for i in range(1, 8):
                whole = whole + buf[i]
            return whole

        return total

    scale_buf[...] = lax.rsqrt(over_col(norm_buf, 0)() + epsilon)
    scale_i = scale_buf[0:1, :]
    scale_t = scale_buf[1:2, :]

    ts_buf[...] = (tx_ref[...] * scale_t).astype(BF16)
    own_cols = pl.ds(pl.multiple_of(z * 128, 128), 128)
    text_sends = []
    for s in range(4):
        copy = remote(
            ts_buf.at[:, pl.ds(s * 128, 128)],
            txt.at[pl.ds(pl.multiple_of(c * SHARE, 16), SHARE), own_cols],
            a2a_sems.at[0, 0, s], a2a_sems.at[0, 1, c % 4], text_to[s],
        )
        copy.start()
        text_sends.append(copy)
    started.append(lambda: [copy.wait_send() for copy in text_sends])

    def rows_of(xx):
        return pl.ds(pl.multiple_of((xx // 2) * SHARE, 16), SHARE)

    def lanes_of(g, xx):
        return pl.ds(pl.multiple_of(g * 256 + (xx % 2) * 128, 128), 128)

    im_low = (im_ref[...] * scale_i).astype(BF16)
    for g in range(4):
        img[y, rows_of(x), lanes_of(g, x)] = im_low[:, g * 128 : g * 128 + 128]

    ways = [[(0, 0, 2), (1, 0, 1)], [(1, 0, 2), (0, 0, 1)]]

    def gather_of(g, phase):
        sems = (g_sems.at[0, g, phase], g_sems.at[1, g, phase])
        if (g + phase) % 2 == 0:
            if phase == 0:
                piece = lambda o, h: img.at[y, rows_of(o), lanes_of(g, o)]
            else:
                piece = lambda o, h: img.at[:, rows_of(o), lanes_of(g, o)]
            return Direct(piece, x, on_x, *sems) if phase == 0 else Gather(piece, x, 4, x_near, ways[g // 2], *sems)
        if phase == 0:
            piece = lambda o, h: img.at[o, rows_of(x), lanes_of(g, x)]
        else:
            piece = lambda o, h: img.at[o, :, pl.ds(g * 256, 256)]
        return Direct(piece, y, on_y, *sems) if phase == 0 else Gather(piece, y, 4, y_near, ways[g // 2], *sems)

    first = [gather_of(g, 0) for g in range(4)]
    second = [gather_of(g, 1) for g in range(4)]

    def text_rows(half, o, h=None):
        start, size = (half * 576, 576) if h is None else (half * 576 + h * 288, 288)
        return txt.at[pl.ds(pl.multiple_of(start, 16), size), pl.ds(pl.multiple_of(o * 128, 128), 128)]

    z_ways = [(0, 0, 4), (1, 1, 4), (1, 0, 3), (0, 1, 3)]
    gz = Gather(lambda o, h: text_rows(fh, o, h), z, 8, z_near, z_ways, gz_sems.at[0], gz_sems.at[1])
    sib_copies = []

    def to_sibling(o, h, slot):
        ref = text_rows(fh, o, h)
        copy = remote(ref, ref, sib_sems.at[0, slot], sib_sems.at[1, slot], sibling)
        copy.start()
        sib_copies.append(copy)

    def from_sibling(o, h, slot):
        ref = text_rows(1 - fh, o, h)
        remote(ref, ref, sib_sems.at[0, slot], sib_sems.at[1, slot], sibling).wait_recv()

    def turn(o):
        cols = pl.ds(pl.multiple_of(o * 128, 128), 128)
        txt_t[cols, :] = txt[:, cols].T

    def turn_step(t):
        for chain in gz.chains(t):
            way, half, n, base = chain
            from_sibling(gz.at(-t - 1 if way == 0 else t + 1), half, base + t)
        turn(gz.at(t + 1))
        if t < 3:
            turn(gz.at(-t - 1))

    lead, trail = [(0, 0), (1, 1)], [(1, 0), (0, 1)]
    for i in range(4):
        ref = txt.at[pl.ds(pl.multiple_of(fh * 576 + i * SHARE, 16), SHARE), own_cols]
        remote(ref, ref, a2a_sems.at[0, 0, i], a2a_sems.at[0, 1, i], sibling).wait_recv()
    far = [[(g // 2, 0)] for g in range(4)]
    near = [[(1 - g // 2, 0)] for g in range(4)]
    gz.send(lead)
    for ring in first:
        ring.send()
    to_sibling(z, None, 14)
    gz.send(trail)
    gz.arrive(0, to_sibling, lead)
    gz.arrive(0, to_sibling, trail)
    for g in range(4):
        first[g].arrive()
        second[g].send(far[g])
    gz.arrive(1, to_sibling, lead)
    from_sibling(z, None, 14)
    turn(z)
    gz.arrive(1, to_sibling, trail)
    for g in range(4):
        second[g].send(near[g])
    turn_step(0)
    gz.arrive(2, to_sibling, lead)
    second[0].arrive(0, None, far[0])
    second[1].arrive(0, None, far[1])
    second[2].arrive(0, None, far[2])
    second[3].arrive(0, None, far[3])
    gz.arrive(2, to_sibling, trail)
    turn_step(1)
    gz.arrive(3, to_sibling)
    turn_step(2)
    second[0].arrive(0, None, near[0])
    second[1].arrive(0, None, near[1])
    second[0].arrive(1)
    second[1].arrive(1)

    temper = jnp.exp(knob_ref[0:1, :])
    bias_value = knob_ref[1:2, :]
    sum_buf[0] = jnp.zeros((3, 8, 128), F32)

    def fold(v):
        v = jnp.sum(v.reshape(32, 8, 256), axis=0)
        return v[:, 0:128] + v[:, 128:256]

    def fold_growth(e):
        e = e.reshape(32, 8, 256)
        while e.shape[0] > 1:
            half = e.shape[0] // 2
            e = e[:half] + e[half:] + e[:half] * e[half:]
        one, two = e[0, :, 0:128], e[0, :, 128:256]
        return one + two + one * two

    def tile(g, p, labels_far):
        o_1 = (z + 7 - p) % 8 if labels_far else z
        o_2 = (z + 1 + p) % 8
        rows_1 = pl.ds(pl.multiple_of(o_1 * 128, 128), 128)
        rows_2 = pl.ds(pl.multiple_of(o_2 * 128, 128), 128)
        cols = pl.ds(pl.multiple_of(g * 256, 256), 256)
        images = img[:, :, cols].reshape(FEATURES, 256)
        texts = jnp.concatenate([txt_t[rows_1, :], txt_t[rows_2, :]], axis=0)

        def finish(labelled):
            scores = jnp.dot(texts, images, preferred_element_type=F32)
            logits = temper * scores + bias_value
            if labelled:
                row = lax.broadcasted_iota(jnp.int32, (256, 256), 0)
                col = lax.broadcasted_iota(jnp.int32, (256, 256), 1)
                same = col == row + xlo * 128
                same = jnp.logical_and(same, row < 128)
                logits = jnp.where(same, -logits, logits)
            e = jnp.exp(-jnp.abs(logits))
            r = 1.0 / (1.0 + e)
            slopes = jnp.where(logits >= 0, r, e * r)
            if labelled:
                slopes = jnp.where(same, -slopes, slopes)
            low = (temper * slopes).astype(BF16)
            wgt[rows_1, cols] = low[0:128]
            wgt[rows_2, cols] = low[128:256]
            sum_buf[0, 0] += fold(jnp.maximum(logits, 0.0)) + jnp.log1p(fold_growth(e))
            sum_buf[0, 1] += fold(slopes * scores)
            sum_buf[0, 2] += fold(slopes)

        if labels_far:
            finish(False)
        else:
            labelled = jnp.logical_and(c // 4 == k, c % 4 == g)
            pl.when(labelled)(lambda: finish(True))
            pl.when(jnp.logical_not(labelled))(lambda: finish(False))

    def early_tiles(g):
        def body(p, _):
            tile(g, p, True)
            return 0

        lax.fori_loop(0, 3, body, 0)

    def image_part(g):
        part = jnp.dot(txt[...], wgt[:, g * 256 : g * 256 + 256], preferred_element_type=F32)
        for yy in range(4):
            for xx in range(4):
                row = yy * 288 + (xx // 2) * SHARE
                piece = part[row : row + SHARE, (xx % 2) * 128 : (xx % 2) * 128 + 128]
                if g % 2 == 0:
                    gi[g, yy, xx] = piece
                else:
                    gi[g, xx, yy] = piece

    def scatter_of(g, phase):
        sems = (s_sems.at[0, g, phase], s_sems.at[1, g, phase])
        even = g % 2 == 0
        if phase == 0:
            ring = (y, 4, y_near) if even else (x, 4, x_near)
            return Scatter(lambda o, h: gi.at[g, o], *ring, ways[g // 2], *sems, land_1.at[g])
        ring = (x, on_x) if even else (y, on_y)
        return Direct(lambda o, h: gi.at[g, y if even else x, o], *ring, *sems, land_2.at[g])

    back_1 = [scatter_of(g, 0) for g in range(4)]
    back_2 = [scatter_of(g, 1) for g in range(4)]

    early_tiles(0)
    early_tiles(1)
    turn_step(3)
    tile(0, 3, False)
    tile(1, 3, False)
    for g in (2, 3):
        second[g].arrive(0, None, near[g])
        second[g].arrive(1)
    early_tiles(2)
    tile(2, 3, False)
    early_tiles(3)
    tile(3, 3, False)

    def total_stage(stage, base, peers):
        copies = []
        for i, peer in enumerate(peers):
            copies.append(remote(
                sum_buf.at[base], sum_buf.at[base + 1 + i],
                total_sems.at[0, stage, i], total_sems.at[1, stage, i], peer,
            ))
        for copy in copies:
            copy.start()

        def done():
            for copy in copies:
                copy.wait()
            total = sum_buf[base]
            for i in range(len(peers)):
                total = total + sum_buf[base + 1 + i]
            sum_buf[base + 1 + len(peers)] = total

        return done

    s_sib = total_stage(0, 0, [sibling])

    own_half = pl.ds(pl.multiple_of(fh * 576, 8), 576)
    sib_half = pl.ds(pl.multiple_of((1 - fh) * 576, 8), 576)
    pairs = [(4, 3), (-3, 2), (-2, 1), (-1, 0)]
    pair_copies = []

    def text_part(q):
        o_1, o_2 = (z + pairs[q][0] + 8) % 8, (z + pairs[q][1] + 8) % 8
        rows_1 = pl.ds(pl.multiple_of(o_1 * 128, 128), 128)
        rows_2 = pl.ds(pl.multiple_of(o_2 * 128, 128), 128)
        weights = jnp.concatenate([wgt[rows_1, :], wgt[rows_2, :]], axis=0)
        part = lax.dot_general(img[...].reshape(FEATURES, 1024), weights, NT, preferred_element_type=F32)
        gt[2 * q] = part[:, 0:128]
        gt[2 * q + 1] = part[:, 128:256]
        copy = remote(
            gt.at[pl.ds(2 * q, 2), sib_half, :], sib_buf.at[pl.ds(2 * q, 2)],
            pair_sems.at[0, q], pair_sems.at[1, q], sibling,
        )
        copy.start()
        pair_copies.append(copy)

    def join(q):
        pair_copies[q].wait_recv()
        for i in (2 * q, 2 * q + 1):
            gt[i, own_half] = gt[i, own_half] + sib_buf[i]

    offsets = [o % 8 for pair in pairs for o in pair]

    sz = Scatter(
        lambda o, h: gt.at[offsets.index(o), pl.ds(pl.multiple_of(fh * 576 + h * 288, 8), 288)],
        0, 8, z_near, z_ways, sz_sems.at[0], sz_sems.at[1], land_z,
    )

    gs = Gather(
        lambda o, h: sum_z.at[o], z, 8, z_near, [(0, 0, 4), (1, 0, 3)], gs_sems.at[0], gs_sems.at[1]
    )
    text_part(0)
    text_part(1)
    image_part(0)
    back_1[0].send()
    join(0)
    sz.send(lead)
    s_sib()
    s_x = total_stage(1, 2, [x_other])
    image_part(1)
    back_1[1].send()
    sz.send([(0, 1)])
    join(1)
    sz.send([(1, 0)])
    text_part(2)
    s_x()
    sum_z[z] = sum_buf[4]
    gs.send()
    image_part(2)
    back_1[2].send()
    sz.arrive(0, lead)
    text_part(3)
    back_1[0].arrive(0, far[0])
    image_part(3)
    back_1[3].send()
    join(2)
    sz.arrive(0, trail)
    gs.arrive(0)
    back_1[1].arrive(0, far[1])
    join(3)
    sz.arrive(1, lead)
    gs.arrive(1)
    back_1[0].arrive(0, near[0])
    back_1[1].arrive(0, near[1])
    back_1[2].arrive(0, far[2])
    sz.arrive(1, trail)
    gs.arrive(2)
    back_1[3].arrive(0, far[3])
    for ring in first + second + [gz]:
        ring.finish()
    for copy in sib_copies:
        copy.wait_send()
    sz.arrive(2, lead)
    gs.arrive(3)
    total = sum_z[0]
    for i in range(1, 8):
        total = total + sum_z[i]
    sum_buf[5] = total
    s_col = total_stage(2, 5, col_peers)
    back_1[0].arrive(1)
    back_2[0].send()
    back_1[1].arrive(1)
    back_2[1].send()
    sz.arrive(2, trail)
    back_1[2].arrive(0, near[2])
    back_1[3].arrive(0, near[3])
    back_1[2].arrive(1)
    back_2[2].send()
    s_col()
    total = sum_buf[13]
    pairs_inv = 1.0 / float(16384 * 16384)
    for i in range(3):
        mean = jnp.sum(jnp.sum(total[i], axis=0, keepdims=True), axis=1, keepdims=True) * pairs_inv
        mean_ref[i : i + 1, :] = jnp.broadcast_to(mean, (1, 128)) * (temper[:, 0:128] if i == 1 else 1.0)
    sz.arrive(3)

    back = []
    for i in range(4):
        copy = remote(
            gt.at[7, pl.ds(pl.multiple_of(fh * 576 + i * SHARE, 8), SHARE), :],
            tg.at[:, pl.ds(pl.multiple_of((c % 4) * 128, 128), 128)],
            a2a_sems.at[1, 0, i], a2a_sems.at[1, 1, c % 4], text_from[i],
        )
        copy.start()
        back.append(copy)
    back_1[3].arrive(1)
    back_2[3].send()

    def image_sum(g):
        return gi[g, y, x] if g % 2 == 0 else gi[g, x, y]

    def image_dot(g):
        back_2[g].arrive()
        cols = slice(g * 128, g * 128 + 128)
        unit = im_ref[:, cols] * scale_buf[0:1, cols]
        dot_buf[0, c, 0:1, cols] = jnp.sum(unit * image_sum(g), axis=0, keepdims=True)

    image_dot(0)
    image_dot(1)
    for s in range(4):
        ref = tg.at[:, pl.ds(s * 128, 128)]
        remote(ref, ref, a2a_sems.at[1, 0, s], a2a_sems.at[1, 1, s], sibling).wait_recv()
    dot_buf[1, c, 0:1, :] = jnp.sum(tx_ref[...] * scale_buf[1:2, :] * tg[...], axis=0, keepdims=True)
    text_dots = over_col(dot_buf.at[1], 2)
    image_dot(2)
    image_dot(3)
    image_dots = over_col(dot_buf.at[0], 1)
    for copy in pair_copies + back:
        copy.wait_send()
    for ring in back_1 + back_2 + [sz, gs]:
        ring.finish()
    dots = text_dots()
    scale_t = scale_buf[1:2, :]
    gt_ref[...] = scale_t * (tg[...] - tx_ref[...] * scale_t * dots[0:1, :])
    dots = image_dots()
    for g in range(4):
        cols = slice(g * 128, g * 128 + 128)
        scale = scale_buf[0:1, cols]
        gi_ref[:, cols] = scale * (image_sum(g) - im_ref[:, cols] * scale * dots[0:1, cols])

    finish_all(started)


def hand_over(mean_ref, gi_in, gt_in, loss_ref, gi_out, gt_out, glt_ref, gb_ref, sems):
    copies = [
        pltpu.make_async_copy(gi_in, gi_out, sems.at[0]),
        pltpu.make_async_copy(gt_in, gt_out, sems.at[1]),
    ]
    for copy in copies:
        copy.start()
    loss_ref[0] = mean_ref[0, 0]
    glt_ref[0] = mean_ref[1, 0]
    gb_ref[0] = mean_ref[2, 0]
    for copy in copies:
        copy.wait()


def per_device(images, texts, log_temp, bias, cid=0, name="contrastive"):
    vmem = pl.BlockSpec(memory_space=pltpu.VMEM)
    smem = pl.BlockSpec(memory_space=pltpu.SMEM)
    anywhere = pl.BlockSpec(memory_space=pl.ANY)
    one = jax.ShapeDtypeStruct((1,), F32)
    grad = jax.ShapeDtypeStruct((SHARE, PAIRS), F32)
    scratch = [
        pltpu.VMEM((8, 8, PAIRS), F32),
        pltpu.VMEM((2, 8, 8, PAIRS), F32),
        pltpu.VMEM((8, PAIRS), F32),
        pltpu.VMEM((SHARE, PAIRS), BF16),
        pltpu.VMEM((4, 2 * SHARE, 1024), BF16),
        pltpu.VMEM((FEATURES, 1024), BF16),
        pltpu.VMEM((1024, FEATURES), BF16),
        pltpu.VMEM((1024, 1024), BF16),
        pltpu.VMEM((4, 4, 4, SHARE, 128), F32),
        pltpu.VMEM((8, FEATURES, 128), F32),
        pltpu.VMEM((8, 576, 128), F32),
        pltpu.VMEM((4, 3, 4, SHARE, 128), F32),
        pltpu.VMEM((4, 3, SHARE, 128), F32),
        pltpu.VMEM((14, 288, 128), F32),
        pltpu.VMEM((14, 3, 8, 128), F32),
        pltpu.VMEM((8, 3, 8, 128), F32),
        pltpu.VMEM((SHARE, PAIRS), F32),
        DMA((3, 2, 7)),
        DMA((2, 2, 4)),
        DMA((2, 15)),
        DMA((2, 4)),
        DMA((2, 4, 2, 3)),
        DMA((2, 14)),
        DMA((2, 4, 2, 3)),
        DMA((2, 14)),
        DMA((2, 7)),
        DMA((2, 3, 7)),
    ]
    row = lax.broadcasted_iota(jnp.int32, (8, 256), 0)
    knobs = jnp.where(row == 0, log_temp, bias)
    means = jax.ShapeDtypeStruct((8, 128), F32)
    parts = pl.pallas_call(
        kernel,
        out_shape=(means, grad, grad),
        in_specs=[vmem] * 3,
        out_specs=[vmem] * 3,
        scratch_shapes=scratch,
        compiler_params=pltpu.CompilerParams(
            collective_id=cid, has_side_effects=True, vmem_limit_bytes=38 * 2**20
        ),
        name=name,
    )(images, texts, knobs)
    return pl.pallas_call(
        hand_over,
        out_shape=(one, grad, grad, one, one),
        in_specs=[vmem] * 3,
        out_specs=[smem, anywhere, anywhere, smem, smem],
        scratch_shapes=[DMA((2,))],
        compiler_params=pltpu.CompilerParams(vmem_limit_bytes=4 * 2**20),
        name="hand_over",
    )(*parts)


def solution(mesh):
    in_specs = (P("col", "blk"), P("col", "blk"), P(), P())
    out_specs = (P(), P("col", "blk"), P("col", "blk"), P(), P())
    return jax.shard_map(
        per_device, mesh=mesh, in_specs=in_specs, out_specs=out_specs, check_vma=False
    )
```

```python
import functools

import jax
import jax.numpy as jnp
from jax import lax
from jax.experimental import pallas as pl
from jax.experimental.pallas import tpu as pltpu
from jax.sharding import PartitionSpec as P

epsilon = 1e-06
F32 = jnp.float32
BF16 = jnp.bfloat16
MESH = pl.DeviceIdType.MESH
FEATURES = 1152
NT = (((1,), (1,)), ((), ()))
SHARE = 144
PAIRS = 512
DMA = pltpu.SemaphoreType.DMA


def device(x, y, z, core):
    return ((x % 2) * 16 + z * 2 + core, y * 2 + x // 2)


class Ring:
    def __init__(self, piece, place, size, neighbour, chains, sems, whole, landed=None):
        self.piece, self.place, self.size, self.neighbour = piece, place, size, neighbour
        self.sent, self.recvs = sems
        self.whole, self.landed = whole, landed
        self.all = []
        base = 0
        for way, half, n in chains:
            self.all.append((way, half, n, base))
            base += n

    def at(self, offset):
        return (self.place + offset + 2 * self.size) % self.size

    def chains(self, t, only):
        return [chain for chain in self.all if t < chain[2] and (only is None or chain[:2] in only)]

    def remote(self, chain, t, src, dst):
        way, _, _, base = chain
        return pltpu.make_async_remote_copy(
            src_ref=src, dst_ref=dst, send_sem=self.sent, recv_sem=self.recvs.at[base + t],
            device_id=self.neighbour[way], device_id_type=MESH,
        )

    def send(self, only=None):
        for chain in self.chains(0, only):
            self.copy(chain, 0).start()

    def finish(self):
        self.remote(self.all[0], 0, self.whole, self.whole).wait_send()


class Gather(Ring):
    def copy(self, chain, t):
        way, half = chain[:2]
        ref = self.piece(self.at(-t if way == 0 else t), half)
        return self.remote(chain, t, ref, ref)

    def arrive(self, t, only=None, then=None):
        for chain in self.chains(t, only):
            way, half, n, base = chain
            owner = self.at(-t - 1 if way == 0 else t + 1)
            ref = self.piece(owner, half)
            self.remote(chain, t, ref, ref).wait_recv()
            if t + 1 < n:
                self.copy(chain, t + 1).start()
            if then is not None:
                then(owner, 1 + 2 * t + way)


class Scatter(Ring):
    def copy(self, chain, t):
        way, half, n, base = chain
        if t == 0:
            src = self.piece(self.at(n if way == 0 else -n), half)
        else:
            src = self.landed(base + t - 1, half)
        return self.remote(chain, t, src, self.landed(base + t, half))

    def arrive(self, t, only=None):
        for chain in self.chains(t, only):
            way, half, n, base = chain
            self.copy(chain, t).wait_recv()
            ahead = n - t - 1
            own = self.piece(self.at(ahead if way == 0 else -ahead), half)
            slot = self.landed(base + t, half)
            if ahead > 0:
                slot[...] = slot[...] + own[...]
                self.copy(chain, t + 1).start()
            else:
                own[...] = own[...] + slot[...]


class Direct:
    def __init__(self, piece, place, axis, sems, whole, landed=None):
        self.piece, self.place, self.axis = piece, place, axis
        self.sent, self.received = sems
        self.whole, self.landed = whole, landed

    def remote(self, src, dst, i):
        return pltpu.make_async_remote_copy(
            src_ref=src, dst_ref=dst, send_sem=self.sent, recv_sem=self.received,
            device_id=self.axis(i + 1), device_id_type=MESH,
        )

    def send(self):
        for i in (1, 0, 2):
            if self.landed is None:
                src = dst = self.piece(self.place)
            else:
                src, dst = self.piece((self.place + i + 1) % 4), self.landed.at[i]
            self.remote(src, dst, i).start()

    def arrive(self):
        self.remote(self.whole, self.whole, 0).wait_recv()
        if self.landed is not None:
            own = self.piece(self.place)
            own[...] = own[...] + (self.landed[0] + self.landed[1] + self.landed[2])

    def finish(self):
        self.remote(self.whole, self.whole, 0).wait_send()


def finish_all(started):
    for finish in started:
        finish()


def kernel(
    im_ref, tx_ref, knob_ref,
    mean_ref, gi_ref, gt_ref,
    norm_buf, dot_buf, scale_buf, ts_buf, img, txt, txt_t, wgt, gi, gt, sib_buf,
    land_1, land_2, land_z, sum_buf, tg,
    col_sems, a2a_sems, sib_sent, sib_sems, pair_sent, pair_sems, first_sems, g_sent, g_sems, gz_sent, gz_sems,
    s_sent, s_sems, back_sems, sz_sent, sz_sems, total_sems,
):
    b = lax.axis_index("blk")
    c = lax.axis_index("col")
    xlo, z, k = b // 16, (b // 2) % 8, b % 2
    y, xhi = c // 2, c % 2
    x = xhi * 2 + xlo
    fh = 1 - k
    sibling = device(x, y, z, 1 - k)
    x_near = [device((x + 1) % 4, y, z, k), device((x + 3) % 4, y, z, k)]
    y_near = [device(x, (y + 1) % 4, z, k), device(x, (y + 3) % 4, z, k)]
    on_x = lambda i: device((x + i) % 4, y, z, k)
    on_y = lambda i: device(x, (y + i) % 4, z, k)
    z_near = [device(x, y, (z + 1) % 8, k), device(x, y, (z + 7) % 8, k)]
    x_other = device(xhi * 2 + 1 - xlo, y, z, k)
    col_peers = [(b, (c + i) % 8) for i in range(1, 8)]
    across = [(xlo * 16 + z * 2 + 1 - k, 4 * (c // 4) + i) for i in range(4)]
    text_to = [(xlo * 16 + z * 2 + 1 - c // 4, 4 * k + s) for s in range(4)]
    text_from = [(xlo * 16 + z * 2 + c // 4, 4 * fh + i) for i in range(4)]
    started = []

    barrier = pltpu.get_barrier_semaphore()
    greeted = across + x_near + z_near + col_peers
    for peer in greeted:
        pl.semaphore_signal(barrier, inc=1, device_id=peer, device_id_type=MESH)

    def remote(src, dst, send_sem, recv_sem, peer):
        return pltpu.make_async_remote_copy(
            src_ref=src, dst_ref=dst, send_sem=send_sem, recv_sem=recv_sem, device_id=peer, device_id_type=MESH
        )

    im = im_ref[...]
    tx = tx_ref[...]
    norm_buf[c, 0:1, :] = jnp.sum(im * im, axis=0, keepdims=True)
    norm_buf[c, 1:2, :] = jnp.sum(tx * tx, axis=0, keepdims=True)
    pl.semaphore_wait(barrier, len(greeted))

    def over_col(buf, stage):
        for i in range(7):
            remote(buf.at[c], buf.at[c], col_sems.at[stage, 0], col_sems.at[stage, 1], col_peers[i]).start()
        seven = buf.at[pl.ds(0, 7)]
        every = remote(seven, seven, col_sems.at[stage, 0], col_sems.at[stage, 1], col_peers[0])
        started.append(every.wait_send)

        def total():
            every.wait_recv()
            whole = buf[0]
            for i in range(1, 8):
                whole = whole + buf[i]
            return whole

        return total

    scale_buf[...] = lax.rsqrt(over_col(norm_buf, 0)() + epsilon)
    scale_i = scale_buf[0:1, :]
    scale_t = scale_buf[1:2, :]

    ts_buf[...] = (tx_ref[...] * scale_t).astype(BF16)
    own_cols = pl.ds(pl.multiple_of(z * 128, 128), 128)
    for s in range(4):
        remote(
            ts_buf.at[:, pl.ds(s * 128, 128)],
            txt.at[pl.ds(pl.multiple_of(c * SHARE, 16), SHARE), own_cols],
            a2a_sems.at[0, 0], a2a_sems.at[0, 1], text_to[s],
        ).start()
    texts_here = remote(ts_buf, ts_buf, a2a_sems.at[0, 0], a2a_sems.at[0, 1], sibling)
    started.append(texts_here.wait_send)

    def rows_of(xx):
        return pl.ds(pl.multiple_of((xx // 2) * SHARE, 16), SHARE)

    def lanes_of(g, xx):
        return pl.ds(pl.multiple_of(g % 2 * 256 + (xx % 2) * 128, 128), 128)

    im_low = (im_ref[...] * scale_i).astype(BF16)
    for g in range(4):
        img[g // 2, y, rows_of(x), lanes_of(g, x)] = im_low[:, g * 128 : g * 128 + 128]

    ways = [[(0, 0, 2), (1, 0, 1)], [(1, 0, 2), (0, 0, 1)]]
    far = [[(g // 2, 0)] for g in range(4)]
    near = [[(1 - g // 2, 0)] for g in range(4)]

    first_whole = img.at[:, 0, pl.ds(0, SHARE), pl.ds(0, 384)]
    first = [
        Direct(
            lambda o: img.at[:, y, rows_of(o), lanes_of(0, o)], x, on_x,
            (first_sems.at[0, 0], first_sems.at[0, 1]), first_whole,
        ),
        Direct(
            lambda o: img.at[:, o, rows_of(x), lanes_of(1, x)], y, on_y,
            (first_sems.at[1, 0], first_sems.at[1, 1]), first_whole,
        ),
    ]

    def second_of(g):
        sems = (g_sent.at[g], g_sems.at[g])
        whole = img.at[0, pl.ds(0, 3), :, pl.ds(0, 256)]
        if g % 2 == 0:
            piece = lambda o, h: img.at[g // 2, o, :, pl.ds(0, 256)]
            return Gather(piece, y, 4, y_near, ways[g // 2], sems, whole)
        piece = lambda o, h: img.at[g // 2, :, rows_of(o), lanes_of(g, o)]
        return Gather(piece, x, 4, x_near, ways[g // 2], sems, whole)

    second = [second_of(g) for g in range(4)]

    def text_rows(half, o, h=None):
        start, size = (half * 576, 576) if h is None else (half * 576 + h * 288, 288)
        return txt.at[pl.ds(pl.multiple_of(start, 16), size), pl.ds(pl.multiple_of(o * 128, 128), 128)]

    z_ways = [(0, 0, 4), (1, 1, 4), (1, 0, 3), (0, 1, 3)]
    lead, trail = [(0, 0), (1, 1)], [(1, 0), (0, 1)]
    gz = Gather(
        lambda o, h: text_rows(fh, o, h), z, 8, z_near, z_ways, (gz_sent.at[0], gz_sems),
        txt.at[pl.ds(0, 576), pl.ds(0, 896)],
    )

    def to_sibling(o, slot):
        ref = text_rows(fh, o)
        remote(ref, ref, sib_sent.at[0], sib_sems.at[slot], sibling).start()

    def turn(o, slot):
        ref = text_rows(1 - fh, o)
        remote(ref, ref, sib_sent.at[0], sib_sems.at[slot], sibling).wait_recv()
        cols = pl.ds(pl.multiple_of(o * 128, 128), 128)
        txt_t[cols, :] = txt[:, cols].T

    def turn_step(t):
        turn(gz.at(-t - 1), 1 + 2 * t)
        if t < 3:
            turn(gz.at(t + 1), 2 + 2 * t)

    texts_here.wait_recv()
    gz.send(lead)
    for ring in first:
        ring.send()
    gz.send(trail)
    to_sibling(z, 0)
    gz.arrive(0, lead)
    gz.arrive(0, trail, to_sibling)
    first[0].arrive()
    second[0].send(far[0])
    second[2].send(far[2])
    first[1].arrive()
    second[1].send(far[1])
    second[3].send(far[3])
    gz.arrive(1, lead)
    turn(z, 0)
    gz.arrive(1, trail, to_sibling)
    for g in range(4):
        second[g].send(near[g])
    turn_step(0)
    gz.arrive(2, lead)
    for g in range(4):
        second[g].arrive(0, far[g])
    gz.arrive(2, trail, to_sibling)
    turn_step(1)
    gz.arrive(3)
    to_sibling(gz.at(4), 7)
    turn_step(2)
    for g in range(2):
        second[g].arrive(0, near[g])
        second[g].arrive(1)

    temper = jnp.exp(knob_ref[0:1, :])
    bias_value = knob_ref[1:2, :]
    sum_buf[0] = jnp.zeros((3, 8, 128), F32)

    def fold(v):
        v = jnp.sum(v.reshape(32, 8, 256), axis=0)
        return v[:, 0:128] + v[:, 128:256]

    def fold_growth(e):
        e = e.reshape(32, 8, 256)
        while e.shape[0] > 1:
            half = e.shape[0] // 2
            e = e[:half] + e[half:] + e[:half] * e[half:]
        one, two = e[0, :, 0:128], e[0, :, 128:256]
        return one + two + one * two

    def tile(g, p, labels_far):
        o_1 = (z + 7 - p) % 8 if labels_far else z
        o_2 = (z + 1 + p) % 8
        rows_1 = pl.ds(pl.multiple_of(o_1 * 128, 128), 128)
        rows_2 = pl.ds(pl.multiple_of(o_2 * 128, 128), 128)
        cols = pl.ds(pl.multiple_of(g * 256, 256), 256)
        images = img[g // 2, :, :, g % 2 * 256 : g % 2 * 256 + 256].reshape(FEATURES, 256)
        texts = jnp.concatenate([txt_t[rows_1, :], txt_t[rows_2, :]], axis=0)

        def finish(labelled):
            scores = jnp.dot(texts, images, preferred_element_type=F32)
            logits = temper * scores + bias_value
            if labelled:
                row = lax.broadcasted_iota(jnp.int32, (256, 256), 0)
                col = lax.broadcasted_iota(jnp.int32, (256, 256), 1)
                same = col == row + xlo * 128
                same = jnp.logical_and(same, row < 128)
                logits = jnp.where(same, -logits, logits)
            e = jnp.exp(-jnp.abs(logits))
            r = 1.0 / (1.0 + e)
            slopes = jnp.where(logits >= 0, r, e * r)
            if labelled:
                slopes = jnp.where(same, -slopes, slopes)
            low = (temper * slopes).astype(BF16)
            wgt[rows_1, cols] = low[0:128]
            wgt[rows_2, cols] = low[128:256]
            sum_buf[0, 0] += fold(jnp.maximum(logits, 0.0)) + jnp.log1p(fold_growth(e))
            sum_buf[0, 1] += fold(slopes * scores)
            sum_buf[0, 2] += fold(slopes)

        if labels_far:
            finish(False)
        else:
            labelled = jnp.logical_and(c // 4 == k, c % 4 == g)
            pl.when(labelled)(lambda: finish(True))
            pl.when(jnp.logical_not(labelled))(lambda: finish(False))

    def early_tiles(g):
        def body(p, _):
            tile(g, p, True)
            return 0

        lax.fori_loop(0, 3, body, 0)

    def image_part(g):
        part = jnp.dot(txt[...], wgt[:, g * 256 : g * 256 + 256], preferred_element_type=F32)
        for yy in range(4):
            for xx in range(4):
                row = yy * 288 + (xx // 2) * SHARE
                piece = part[row : row + SHARE, (xx % 2) * 128 : (xx % 2) * 128 + 128]
                if g % 2 == 0:
                    gi[g, yy, xx] = piece
                else:
                    gi[g, xx, yy] = piece

    def back_1_of(g):
        ring = (y, 4, y_near) if g % 2 == 0 else (x, 4, x_near)
        return Scatter(
            lambda o, h: gi.at[g, o], *ring, ways[g // 2], (s_sent.at[g], s_sems.at[g]), land_1.at[g],
            lambda i, h: land_1.at[g, i],
        )

    def back_2_of(g):
        ring = (x, on_x) if g % 2 == 0 else (y, on_y)
        return Direct(
            lambda o: gi.at[g, y if g % 2 == 0 else x, o], *ring, (back_sems.at[0, g], back_sems.at[1, g]),
            land_2.at[g], land_2.at[g],
        )

    back_1 = [back_1_of(g) for g in range(4)]
    back_2 = [back_2_of(g) for g in range(4)]

    early_tiles(0)
    early_tiles(1)
    turn_step(3)
    tile(0, 3, False)
    tile(1, 3, False)
    for g in (2, 3):
        second[g].arrive(0, near[g])
        second[g].arrive(1)
    early_tiles(2)
    tile(2, 3, False)
    early_tiles(3)
    tile(3, 3, False)

    def total_stage(stage, base, peers):
        copies = []
        for i, peer in enumerate(peers):
            copies.append(remote(
                sum_buf.at[base], sum_buf.at[base + 1 + i],
                total_sems.at[0, stage, i], total_sems.at[1, stage, i], peer,
            ))
        for copy in copies:
            copy.start()

        def done():
            for copy in copies:
                copy.wait()
            total = sum_buf[base]
            for i in range(len(peers)):
                total = total + sum_buf[base + 1 + i]
            sum_buf[base + 1 + len(peers)] = total

        return done

    s_sib = total_stage(0, 0, [sibling])

    own_half = pl.ds(pl.multiple_of(fh * 584 + 8, 8), 576)
    sib_half = pl.ds(pl.multiple_of((1 - fh) * 584 + 8, 8), 576)
    sum_rows = pl.ds(pl.multiple_of(fh * 584, 8), 8)
    pairs = [(4, 3), (-3, 2), (-2, 1), (-1, 0)]

    def text_part(q):
        o_1, o_2 = (z + pairs[q][0] + 8) % 8, (z + pairs[q][1] + 8) % 8
        rows_1 = pl.ds(pl.multiple_of(o_1 * 128, 128), 128)
        rows_2 = pl.ds(pl.multiple_of(o_2 * 128, 128), 128)
        weights = jnp.concatenate([wgt[rows_1, :], wgt[rows_2, :]], axis=0)
        part = lax.dot_general(
            img[0].reshape(FEATURES, 512), weights[:, 0:512], NT, preferred_element_type=F32
        ) + lax.dot_general(img[1].reshape(FEATURES, 512), weights[:, 512:1024], NT, preferred_element_type=F32)
        for i in range(2):
            for f in range(2):
                gt[2 * q + i, f * 584 + 8 : f * 584 + 584] = part[f * 576 : f * 576 + 576, i * 128 : i * 128 + 128]
        pair_copy(q).start()

    def pair_copy(q):
        return remote(
            gt.at[pl.ds(2 * q, 2), sib_half, :], sib_buf.at[pl.ds(2 * q, 2)],
            pair_sent.at[0], pair_sems.at[q], sibling,
        )

    def join(q):
        pair_copy(q).wait_recv()
        for i in (2 * q, 2 * q + 1):
            gt[i, own_half] = gt[i, own_half] + sib_buf[i]

    offsets = [o % 8 for pair in pairs for o in pair]

    def gt_piece(o, h):
        rows = pl.ds(pl.multiple_of(fh * 584, 8), 296) if h == 0 else pl.ds(pl.multiple_of(fh * 584 + 296, 8), 288)
        return gt.at[offsets.index(o), rows]

    sz = Scatter(
        gt_piece, 0, 8, z_near, z_ways, (sz_sent.at[0], sz_sems), gt.at[pl.ds(0, 7), pl.ds(0, 584)],
        lambda i, h: land_z.at[i, pl.ds(0, 296 if h == 0 else 288)],
    )
    text_part(0)
    s_sib()
    s_x = total_stage(1, 2, [x_other])
    image_part(0)
    back_1[0].send()
    image_part(1)
    back_1[1].send()
    s_x()
    sums = jnp.concatenate([jnp.sum(sum_buf[4, i], axis=0, keepdims=True) for i in range(3)] * 2 + [jnp.zeros((2, 128), F32)])
    for i in range(8):
        gt[i, sum_rows] = sums
    join(0)
    sz.send(lead)
    text_part(1)
    sz.send([(0, 1)])
    image_part(2)
    back_1[2].send()
    join(1)
    sz.send([(1, 0)])
    image_part(3)
    back_1[3].send()
    text_part(2)
    sz.arrive(0, lead)
    back_1[0].arrive(0, far[0])
    text_part(3)
    join(2)
    sz.arrive(0, trail)
    back_1[1].arrive(0, far[1])
    join(3)
    sz.arrive(1, lead)
    back_1[2].arrive(0, far[2])
    back_1[3].arrive(0, far[3])
    sz.arrive(1, trail)
    back_1[0].arrive(0, near[0])
    back_1[1].arrive(0, near[1])
    sz.arrive(2, lead)
    back_1[0].arrive(1)
    back_2[0].send()
    back_1[1].arrive(1)
    back_2[1].send()
    sz.arrive(2, trail)
    back_1[2].arrive(0, near[2])
    back_1[3].arrive(0, near[3])
    back_1[2].arrive(1)
    back_2[2].send()
    sz.arrive(3)

    for i in range(4):
        remote(
            gt.at[7, pl.ds(pl.multiple_of(fh * 584 + 8 + i * SHARE, 8), SHARE), :],
            tg.at[:, pl.ds(pl.multiple_of((c % 4) * 128, 128), 128)],
            a2a_sems.at[1, 0], a2a_sems.at[1, 1], text_from[i],
        ).start()
    grads_here = remote(tg, tg, a2a_sems.at[1, 0], a2a_sems.at[1, 1], sibling)
    started.append(grads_here.wait_send)
    back_1[3].arrive(1)
    back_2[3].send()

    def image_sum(g):
        return gi[g, y, x] if g % 2 == 0 else gi[g, x, y]

    def image_dot(g):
        back_2[g].arrive()
        cols = slice(g * 128, g * 128 + 128)
        unit = im_ref[:, cols] * scale_buf[0:1, cols]
        dot_buf[c, 0:1, cols] = jnp.sum(unit * image_sum(g), axis=0, keepdims=True)

    dot_buf[c, 2:5, 0:128] = gt[7, sum_rows][0:3]
    image_dot(0)
    image_dot(1)
    grads_here.wait_recv()
    dot_buf[c, 1:2, :] = jnp.sum(tx_ref[...] * scale_buf[1:2, :] * tg[...], axis=0, keepdims=True)
    image_dot(2)
    image_dot(3)
    every_dot = over_col(dot_buf, 1)
    pairs_sent = remote(sib_buf, sib_buf, pair_sent.at[0], pair_sems.at[0], sibling)
    texts_sent = remote(txt.at[pl.ds(0, 576), :], txt.at[pl.ds(0, 576), :], sib_sent.at[0], sib_sems.at[0], sibling)
    for copy in (pairs_sent, texts_sent):
        copy.wait_send()
    for ring in first + second + [gz] + back_1 + back_2 + [sz]:
        ring.finish()
    dots = every_dot()
    scale_t = scale_buf[1:2, :]
    gt_ref[...] = scale_t * (tg[...] - tx_ref[...] * scale_t * dots[1:2, :])
    for g in range(4):
        cols = slice(g * 128, g * 128 + 128)
        scale = scale_buf[0:1, cols]
        gi_ref[:, cols] = scale * (image_sum(g) - im_ref[:, cols] * scale * dots[0:1, cols])
    means = jnp.sum(dots[:, 0:128], axis=1, keepdims=True) * (1.0 / float(16384 * 16384))
    mean_ref[...] = jnp.broadcast_to(means, (8, 128))
    mean_ref[3:4, :] = mean_ref[3:4, :] * temper[:, 0:128]

    finish_all(started)


def hand_over(mean_ref, gi_in, gt_in, loss_ref, gi_out, gt_out, glt_ref, gb_ref, sems):
    copies = [
        pltpu.make_async_copy(gi_in, gi_out, sems.at[0]),
        pltpu.make_async_copy(gt_in, gt_out, sems.at[1]),
    ]
    for copy in copies:
        copy.start()
    loss_ref[0] = mean_ref[2, 0]
    glt_ref[0] = mean_ref[3, 0]
    gb_ref[0] = mean_ref[4, 0]
    for copy in copies:
        copy.wait()


def per_device(images, texts, log_temp, bias, cid=0, name="contrastive"):
    vmem = pl.BlockSpec(memory_space=pltpu.VMEM)
    smem = pl.BlockSpec(memory_space=pltpu.SMEM)
    anywhere = pl.BlockSpec(memory_space=pl.ANY)
    one = jax.ShapeDtypeStruct((1,), F32)
    grad = jax.ShapeDtypeStruct((SHARE, PAIRS), F32)
    scratch = [
        pltpu.VMEM((8, 8, PAIRS), F32),
        pltpu.VMEM((8, 8, PAIRS), F32),
        pltpu.VMEM((8, PAIRS), F32),
        pltpu.VMEM((SHARE, PAIRS), BF16),
        pltpu.VMEM((2, 4, 2 * SHARE, 512), BF16),
        pltpu.VMEM((FEATURES, 1024), BF16),
        pltpu.VMEM((1024, FEATURES), BF16),
        pltpu.VMEM((1024, 1024), BF16),
        pltpu.VMEM((4, 4, 4, SHARE, 128), F32),
        pltpu.VMEM((8, 1168, 128), F32),
        pltpu.VMEM((8, 576, 128), F32),
        pltpu.VMEM((4, 3, 4, SHARE, 128), F32),
        pltpu.VMEM((4, 3, SHARE, 128), F32),
        pltpu.VMEM((14, 296, 128), F32),
        pltpu.VMEM((5, 3, 8, 128), F32),
        pltpu.VMEM((SHARE, PAIRS), F32),
        DMA((2, 2)),
        DMA((2, 2)),
        DMA((1,)),
        DMA((8,)),
        DMA((1,)),
        DMA((4,)),
        DMA((2, 2)),
        DMA((4,)),
        DMA((4, 3)),
        DMA((1,)),
        DMA((14,)),
        DMA((4,)),
        DMA((4, 3)),
        DMA((2, 4)),
        DMA((1,)),
        DMA((14,)),
        DMA((2, 2, 1)),
    ]
    row = lax.broadcasted_iota(jnp.int32, (8, 256), 0)
    knobs = jnp.where(row == 0, log_temp, bias)
    means = jax.ShapeDtypeStruct((8, 128), F32)
    parts = pl.pallas_call(
        kernel,
        out_shape=(means, grad, grad),
        in_specs=[vmem] * 3,
        out_specs=[vmem] * 3,
        scratch_shapes=scratch,
        compiler_params=pltpu.CompilerParams(
            collective_id=cid, has_side_effects=True, vmem_limit_bytes=38 * 2**20
        ),
        name=name,
    )(images, texts, knobs)
    return pl.pallas_call(
        hand_over,
        out_shape=(one, grad, grad, one, one),
        in_specs=[vmem] * 3,
        out_specs=[smem, anywhere, anywhere, smem, smem],
        scratch_shapes=[DMA((2,))],
        compiler_params=pltpu.CompilerParams(vmem_limit_bytes=4 * 2**20),
        name="hand_over",
    )(*parts)


def solution(mesh):
    in_specs = (P("col", "blk"), P("col", "blk"), P(), P())
    out_specs = (P(), P("col", "blk"), P("col", "blk"), P(), P())
    return jax.shard_map(
        per_device, mesh=mesh, in_specs=in_specs, out_specs=out_specs, check_vma=False
    )
```

```python
import functools

import jax
import jax.numpy as jnp
from jax import lax
from jax.experimental import pallas as pl
from jax.experimental.pallas import tpu as pltpu
from jax.sharding import PartitionSpec as P

epsilon = 1e-06
F32 = jnp.float32
BF16 = jnp.bfloat16
MESH = pl.DeviceIdType.MESH
FEATURES = 1152
NT = (((1,), (1,)), ((), ()))
SHARE = 144
PAIRS = 512
DMA = pltpu.SemaphoreType.DMA


def device(x, y, z, core):
    return ((x % 2) * 16 + z * 2 + core, y * 2 + x // 2)


class Ring:
    def __init__(self, piece, place, size, neighbour, chains, sems, whole, landed=None):
        self.piece, self.place, self.size, self.neighbour = piece, place, size, neighbour
        self.sent, self.recvs = sems
        self.whole, self.landed = whole, landed
        self.all = []
        base = 0
        for way, half, n in chains:
            self.all.append((way, half, n, base))
            base += n

    def at(self, offset):
        return (self.place + offset + 2 * self.size) % self.size

    def chains(self, t, only):
        return [chain for chain in self.all if t < chain[2] and (only is None or chain[:2] in only)]

    def remote(self, chain, t, src, dst):
        way, _, _, base = chain
        return pltpu.make_async_remote_copy(
            src_ref=src, dst_ref=dst, send_sem=self.sent, recv_sem=self.recvs.at[base + t],
            device_id=self.neighbour[way], device_id_type=MESH,
        )

    def send(self, only=None):
        for chain in self.chains(0, only):
            self.copy(chain, 0).start()

    def finish(self):
        self.remote(self.all[0], 0, self.whole, self.whole).wait_send()


class Gather(Ring):
    def copy(self, chain, t):
        way, half = chain[:2]
        ref = self.piece(self.at(-t if way == 0 else t), half)
        return self.remote(chain, t, ref, ref)

    def arrive(self, t, only=None, then=None):
        for chain in self.chains(t, only):
            way, half, n, base = chain
            owner = self.at(-t - 1 if way == 0 else t + 1)
            ref = self.piece(owner, half)
            self.remote(chain, t, ref, ref).wait_recv()
            if t + 1 < n:
                self.copy(chain, t + 1).start()
            if then is not None:
                then(owner, 1 + 2 * t + way)


class Scatter(Ring):
    def copy(self, chain, t):
        way, half, n, base = chain
        if t == 0:
            src = self.piece(self.at(n if way == 0 else -n), half)
        else:
            src = self.landed(base + t - 1, half)
        return self.remote(chain, t, src, self.landed(base + t, half))

    def arrive(self, t, only=None):
        for chain in self.chains(t, only):
            way, half, n, base = chain
            self.copy(chain, t).wait_recv()
            ahead = n - t - 1
            own = self.piece(self.at(ahead if way == 0 else -ahead), half)
            slot = self.landed(base + t, half)
            if ahead > 0:
                slot[...] = slot[...] + own[...]
                self.copy(chain, t + 1).start()
            else:
                own[...] = own[...] + slot[...]


class Direct:
    def __init__(self, piece, place, axis, sems, whole, landed=None):
        self.piece, self.place, self.axis = piece, place, axis
        self.sent, self.received = sems
        self.whole, self.landed = whole, landed

    def remote(self, src, dst, i):
        return pltpu.make_async_remote_copy(
            src_ref=src, dst_ref=dst, send_sem=self.sent, recv_sem=self.received,
            device_id=self.axis(i + 1), device_id_type=MESH,
        )

    def send(self):
        for i in (1, 0, 2):
            if self.landed is None:
                src = dst = self.piece(self.place)
            else:
                src, dst = self.piece((self.place + i + 1) % 4), self.landed.at[i]
            self.remote(src, dst, i).start()

    def arrive(self):
        self.remote(self.whole, self.whole, 0).wait_recv()
        if self.landed is not None:
            own = self.piece(self.place)
            own[...] = own[...] + (self.landed[0] + self.landed[1] + self.landed[2])

    def finish(self):
        self.remote(self.whole, self.whole, 0).wait_send()


def finish_all(started):
    for finish in started:
        finish()


def kernel(
    im_ref, tx_ref, knob_ref,
    mean_ref, gi_ref, gt_ref,
    norm_buf, dot_buf, scale_buf, ts_buf, img, txt, txt_t, wgt, gi, gt, sib_buf,
    land_1, land_2, land_z, tile_sums, sum_buf, tg,
    col_sems, a2a_sems, sib_sent, sib_sems, pair_sent, pair_sems, first_sems, g_sent, g_sems, gz_sent, gz_sems,
    s_sent, s_sems, back_sems, sz_sent, sz_sems, total_sems,
):
    b = lax.axis_index("blk")
    c = lax.axis_index("col")
    xlo, z, k = b // 16, (b // 2) % 8, b % 2
    y, xhi = c // 2, c % 2
    x = xhi * 2 + xlo
    fh = 1 - k
    sibling = device(x, y, z, 1 - k)
    x_near = [device((x + 1) % 4, y, z, k), device((x + 3) % 4, y, z, k)]
    y_near = [device(x, (y + 1) % 4, z, k), device(x, (y + 3) % 4, z, k)]
    on_x = lambda i: device((x + i) % 4, y, z, k)
    on_y = lambda i: device(x, (y + i) % 4, z, k)
    z_near = [device(x, y, (z + 1) % 8, k), device(x, y, (z + 7) % 8, k)]
    x_other = device(xhi * 2 + 1 - xlo, y, z, k)
    col_peers = [(b, (c + i) % 8) for i in range(1, 8)]
    across = [(xlo * 16 + z * 2 + 1 - k, 4 * (c // 4) + i) for i in range(4)]
    text_to = [(xlo * 16 + z * 2 + 1 - c // 4, 4 * k + s) for s in range(4)]
    text_from = [(xlo * 16 + z * 2 + c // 4, 4 * fh + i) for i in range(4)]
    started = []

    barrier = pltpu.get_barrier_semaphore()
    greeted = across + x_near + z_near + col_peers
    for peer in greeted:
        pl.semaphore_signal(barrier, inc=1, device_id=peer, device_id_type=MESH)

    def remote(src, dst, send_sem, recv_sem, peer):
        return pltpu.make_async_remote_copy(
            src_ref=src, dst_ref=dst, send_sem=send_sem, recv_sem=recv_sem, device_id=peer, device_id_type=MESH
        )

    im = im_ref[...]
    tx = tx_ref[...]
    norm_buf[c, 0:1, :] = jnp.sum(im * im, axis=0, keepdims=True)
    norm_buf[c, 1:2, :] = jnp.sum(tx * tx, axis=0, keepdims=True)
    pl.semaphore_wait(barrier, len(greeted))

    def over_col(buf, stage):
        for i in range(7):
            remote(buf.at[c], buf.at[c], col_sems.at[stage, 0], col_sems.at[stage, 1], col_peers[i]).start()
        seven = buf.at[pl.ds(0, 7)]
        every = remote(seven, seven, col_sems.at[stage, 0], col_sems.at[stage, 1], col_peers[0])
        started.append(every.wait_send)

        def total():
            every.wait_recv()
            whole = buf[0]
            for i in range(1, 8):
                whole = whole + buf[i]
            return whole

        return total

    scale_buf[...] = lax.rsqrt(over_col(norm_buf, 0)() + epsilon)
    scale_i = scale_buf[0:1, :]
    scale_t = scale_buf[1:2, :]

    ts_buf[...] = (tx_ref[...] * scale_t).astype(BF16)
    own_cols = pl.ds(pl.multiple_of(z * 128, 128), 128)
    for s in range(4):
        remote(
            ts_buf.at[:, pl.ds(s * 128, 128)],
            txt.at[pl.ds(pl.multiple_of(c * SHARE, 16), SHARE), own_cols],
            a2a_sems.at[0, 0], a2a_sems.at[0, 1], text_to[s],
        ).start()
    texts_here = remote(ts_buf, ts_buf, a2a_sems.at[0, 0], a2a_sems.at[0, 1], sibling)
    started.append(texts_here.wait_send)

    def rows_of(xx):
        return pl.ds(pl.multiple_of((xx // 2) * SHARE, 16), SHARE)

    def lanes_of(g, xx):
        return pl.ds(pl.multiple_of(g % 2 * 256 + (xx % 2) * 128, 128), 128)

    im_low = (im_ref[...] * scale_i).astype(BF16)
    for g in range(4):
        img[g // 2, y, rows_of(x), lanes_of(g, x)] = im_low[:, g * 128 : g * 128 + 128]

    ways = [[(0, 0, 2), (1, 0, 1)], [(1, 0, 2), (0, 0, 1)]]
    far = [[(g // 2, 0)] for g in range(4)]
    near = [[(1 - g // 2, 0)] for g in range(4)]

    first_whole = img.at[:, 0, pl.ds(0, SHARE), pl.ds(0, 384)]
    first = [
        Direct(
            lambda o: img.at[:, y, rows_of(o), lanes_of(0, o)], x, on_x,
            (first_sems.at[0, 0], first_sems.at[0, 1]), first_whole,
        ),
        Direct(
            lambda o: img.at[:, o, rows_of(x), lanes_of(1, x)], y, on_y,
            (first_sems.at[1, 0], first_sems.at[1, 1]), first_whole,
        ),
    ]

    def second_of(g):
        sems = (g_sent.at[g], g_sems.at[g])
        whole = img.at[0, pl.ds(0, 3), :, pl.ds(0, 256)]
        if g % 2 == 0:
            piece = lambda o, h: img.at[g // 2, o, :, pl.ds(0, 256)]
            return Gather(piece, y, 4, y_near, ways[g // 2], sems, whole)
        piece = lambda o, h: img.at[g // 2, :, rows_of(o), lanes_of(g, o)]
        return Gather(piece, x, 4, x_near, ways[g // 2], sems, whole)

    second = [second_of(g) for g in range(4)]

    def text_rows(half, o, h=None):
        start, size = (half * 576, 576) if h is None else (half * 576 + h * 288, 288)
        return txt.at[pl.ds(pl.multiple_of(start, 16), size), pl.ds(pl.multiple_of(o * 128, 128), 128)]

    z_ways = [(0, 0, 4), (1, 1, 4), (1, 0, 3), (0, 1, 3)]
    lead, trail = [(0, 0), (1, 1)], [(1, 0), (0, 1)]
    gz = Gather(
        lambda o, h: text_rows(fh, o, h), z, 8, z_near, z_ways, (gz_sent.at[0], gz_sems),
        txt.at[pl.ds(0, 576), pl.ds(0, 896)],
    )

    def to_sibling(o, slot):
        ref = text_rows(fh, o)
        remote(ref, ref, sib_sent.at[0], sib_sems.at[slot], sibling).start()

    def turn(o, slot):
        ref = text_rows(1 - fh, o)
        remote(ref, ref, sib_sent.at[0], sib_sems.at[slot], sibling).wait_recv()
        cols = pl.ds(pl.multiple_of(o * 128, 128), 128)
        txt_t[cols, :] = txt[:, cols].T

    def turn_step(t):
        turn(gz.at(-t - 1), 1 + 2 * t)
        if t < 3:
            turn(gz.at(t + 1), 2 + 2 * t)

    for ring in first:
        ring.send()
    texts_here.wait_recv()
    gz.send(lead)
    gz.send(trail)
    to_sibling(z, 0)
    gz.arrive(0, lead)
    gz.arrive(0, trail, to_sibling)
    first[0].arrive()
    second[0].send(far[0])
    second[2].send(far[2])
    first[1].arrive()
    second[1].send(far[1])
    second[3].send(far[3])
    gz.arrive(1, lead)
    turn(z, 0)
    gz.arrive(1, trail, to_sibling)
    for g in range(4):
        second[g].send(near[g])
    turn_step(0)
    gz.arrive(2, lead)
    for g in range(4):
        second[g].arrive(0, far[g])
    gz.arrive(2, trail, to_sibling)
    turn_step(1)
    gz.arrive(3)
    to_sibling(gz.at(4), 7)
    turn_step(2)
    for g in range(2):
        second[g].arrive(0, near[g])
        second[g].arrive(1)

    temper = jnp.exp(knob_ref[0:1, :])
    bias_value = knob_ref[1:2, :]
    tile_sums[...] = jnp.zeros_like(tile_sums)

    def fold(v):
        v = jnp.sum(v.reshape(32, 8, 256), axis=0)
        return v[:, 0:128] + v[:, 128:256]

    def fold_growth(e):
        e = e.reshape(32, 8, 256)
        while e.shape[0] > 1:
            half = e.shape[0] // 2
            e = e[:half] + e[half:] + e[:half] * e[half:]
        one, two = e[0, :, 0:128], e[0, :, 128:256]
        return one + two + one * two

    def tile(g, p, labels_far):
        o_1 = (z + 7 - p) % 8 if labels_far else z
        o_2 = (z + 1 + p) % 8
        rows_1 = pl.ds(pl.multiple_of(o_1 * 128, 128), 128)
        rows_2 = pl.ds(pl.multiple_of(o_2 * 128, 128), 128)
        cols = pl.ds(pl.multiple_of(g * 256, 256), 256)
        images = img[g // 2, :, :, g % 2 * 256 : g % 2 * 256 + 256].reshape(FEATURES, 256)
        texts = jnp.concatenate([txt_t[rows_1, :], txt_t[rows_2, :]], axis=0)

        def finish(labelled):
            scores = jnp.dot(texts, images, preferred_element_type=F32)
            logits = temper * scores + bias_value
            if labelled:
                row = lax.broadcasted_iota(jnp.int32, (256, 256), 0)
                col = lax.broadcasted_iota(jnp.int32, (256, 256), 1)
                same = col == row + xlo * 128
                same = jnp.logical_and(same, row < 128)
                logits = jnp.where(same, -logits, logits)
            e = jnp.exp(-jnp.abs(logits))
            r = 1.0 / (1.0 + e)
            slopes = jnp.where(logits >= 0, r, e * r)
            if labelled:
                slopes = jnp.where(same, -slopes, slopes)
            low = (temper * slopes).astype(BF16)
            wgt[rows_1, cols] = low[0:128]
            wgt[rows_2, cols] = low[128:256]
            tile_sums[0] += fold(jnp.maximum(logits, 0.0)) + jnp.log1p(fold_growth(e))
            tile_sums[1] += fold(slopes * scores)
            tile_sums[2] += fold(slopes)

        if labels_far:
            finish(False)
        else:
            labelled = jnp.logical_and(c // 4 == k, c % 4 == g)
            pl.when(labelled)(lambda: finish(True))
            pl.when(jnp.logical_not(labelled))(lambda: finish(False))

    def early_tiles(g, start=0, stop=3):
        def body(p, _):
            tile(g, p, True)
            return 0

        lax.fori_loop(start, stop, body, 0)

    def image_part(g):
        part = jnp.dot(txt[...], wgt[:, g * 256 : g * 256 + 256], preferred_element_type=F32)
        for yy in range(4):
            for xx in range(4):
                row = yy * 288 + (xx // 2) * SHARE
                piece = part[row : row + SHARE, (xx % 2) * 128 : (xx % 2) * 128 + 128]
                if g % 2 == 0:
                    gi[g, yy, xx] = piece
                else:
                    gi[g, xx, yy] = piece

    def back_1_of(g):
        ring = (y, 4, y_near) if g % 2 == 0 else (x, 4, x_near)
        return Scatter(
            lambda o, h: gi.at[g, o], *ring, ways[g // 2], (s_sent.at[g], s_sems.at[g]), land_1.at[g],
            lambda i, h: land_1.at[g, i],
        )

    def back_2_of(g):
        ring = (x, on_x) if g % 2 == 0 else (y, on_y)
        return Direct(
            lambda o: gi.at[g, y if g % 2 == 0 else x, o], *ring, (back_sems.at[0, g], back_sems.at[1, g]),
            land_2.at[g], land_2.at[g],
        )

    back_1 = [back_1_of(g) for g in range(4)]
    back_2 = [back_2_of(g) for g in range(4)]

    early_tiles(0)
    early_tiles(1)
    turn_step(3)
    tile(0, 3, False)
    tile(1, 3, False)
    for g in (2, 3):
        second[g].arrive(0, near[g])
        second[g].arrive(1)
    for g in (2, 3):
        tile(g, 3, False)
        early_tiles(g, 2, 3)

    def total_stage(stage, base, peers):
        copies = []
        for i, peer in enumerate(peers):
            copies.append(remote(
                sum_buf.at[base], sum_buf.at[base + 1 + i],
                total_sems.at[0, stage, i], total_sems.at[1, stage, i], peer,
            ))
        for copy in copies:
            copy.start()

        def done():
            for copy in copies:
                copy.wait()
            total = sum_buf[base]
            for i in range(len(peers)):
                total = total + sum_buf[base + 1 + i]
            sum_buf[base + 1 + len(peers)] = total

        return done

    own_half = pl.ds(pl.multiple_of(fh * 584 + 8, 8), 576)
    sib_half = pl.ds(pl.multiple_of((1 - fh) * 584 + 8, 8), 576)
    sum_rows = pl.ds(pl.multiple_of(fh * 584, 8), 8)
    pairs = [(4, 3), (-3, 2), (-2, 1), (-1, 0)]

    def text_part(q):
        o_1, o_2 = (z + pairs[q][0] + 8) % 8, (z + pairs[q][1] + 8) % 8
        rows_1 = pl.ds(pl.multiple_of(o_1 * 128, 128), 128)
        rows_2 = pl.ds(pl.multiple_of(o_2 * 128, 128), 128)
        weights = jnp.concatenate([wgt[rows_1, :], wgt[rows_2, :]], axis=0)
        part = lax.dot_general(
            img[0].reshape(FEATURES, 512), weights[:, 0:512], NT, preferred_element_type=F32
        ) + lax.dot_general(img[1].reshape(FEATURES, 512), weights[:, 512:1024], NT, preferred_element_type=F32)
        for i in range(2):
            for f in range(2):
                gt[2 * q + i, f * 584 + 8 : f * 584 + 584] = part[f * 576 : f * 576 + 576, i * 128 : i * 128 + 128]
        pair_copy(q).start()

    def pair_copy(q):
        return remote(
            gt.at[pl.ds(2 * q, 2), sib_half, :], sib_buf.at[pl.ds(2 * q, 2)],
            pair_sent.at[0], pair_sems.at[q], sibling,
        )

    def join(q):
        pair_copy(q).wait_recv()
        for i in (2 * q, 2 * q + 1):
            gt[i, own_half] = gt[i, own_half] + sib_buf[i]

    offsets = [o % 8 for pair in pairs for o in pair]

    def gt_piece(o, h):
        rows = pl.ds(pl.multiple_of(fh * 584, 8), 296) if h == 0 else pl.ds(pl.multiple_of(fh * 584 + 296, 8), 288)
        return gt.at[offsets.index(o), rows]

    sz = Scatter(
        gt_piece, 0, 8, z_near, z_ways, (sz_sent.at[0], sz_sems), gt.at[pl.ds(0, 7), pl.ds(0, 584)],
        lambda i, h: land_z.at[i, pl.ds(0, 296 if h == 0 else 288)],
    )
    text_part(0)
    early_tiles(2, 0, 2)
    early_tiles(3, 0, 2)
    sums = [jnp.sum(tile_sums[i], axis=0, keepdims=True) for i in range(3)]
    sums = jnp.concatenate(sums + [jnp.zeros((5, 128), F32)])
    for i in range(8):
        gt[i, sum_rows] = sums
    image_part(0)
    back_1[0].send()
    text_part(1)
    join(0)
    sz.send(lead)
    image_part(1)
    back_1[1].send()
    sz.send([(0, 1)])
    image_part(2)
    back_1[2].send()
    join(1)
    sz.send([(1, 0)])
    image_part(3)
    back_1[3].send()
    text_part(2)
    sz.arrive(0, lead)
    back_1[0].arrive(0, far[0])
    text_part(3)
    join(2)
    sz.arrive(0, trail)
    back_1[1].arrive(0, far[1])
    join(3)
    sz.arrive(1, lead)
    back_1[2].arrive(0, far[2])
    back_1[3].arrive(0, far[3])
    sz.arrive(1, trail)
    back_1[0].arrive(0, near[0])
    back_1[1].arrive(0, near[1])
    sz.arrive(2, lead)
    back_1[0].arrive(1)
    back_2[0].send()
    back_1[1].arrive(1)
    back_2[1].send()
    sz.arrive(2, trail)
    back_1[2].arrive(0, near[2])
    back_1[3].arrive(0, near[3])
    back_1[2].arrive(1)
    back_2[2].send()
    sz.arrive(3)

    for i in range(4):
        remote(
            gt.at[7, pl.ds(pl.multiple_of(fh * 584 + 8 + i * SHARE, 8), SHARE), :],
            tg.at[:, pl.ds(pl.multiple_of((c % 4) * 128, 128), 128)],
            a2a_sems.at[1, 0], a2a_sems.at[1, 1], text_from[i],
        ).start()
    grads_here = remote(tg, tg, a2a_sems.at[1, 0], a2a_sems.at[1, 1], sibling)
    started.append(grads_here.wait_send)
    sum_buf[0] = gt[7, sum_rows]
    s_sib = total_stage(0, 0, [sibling])
    back_1[3].arrive(1)
    back_2[3].send()
    s_sib()
    s_x = total_stage(1, 2, [x_other])

    def image_sum(g):
        return gi[g, y, x] if g % 2 == 0 else gi[g, x, y]

    def image_dot(g):
        back_2[g].arrive()
        cols = slice(g * 128, g * 128 + 128)
        unit = im_ref[:, cols] * scale_buf[0:1, cols]
        dot_buf[c, 0:1, cols] = jnp.sum(unit * image_sum(g), axis=0, keepdims=True)

    image_dot(0)
    image_dot(1)
    grads_here.wait_recv()
    dot_buf[c, 1:2, :] = jnp.sum(tx_ref[...] * scale_buf[1:2, :] * tg[...], axis=0, keepdims=True)
    s_x()
    dot_buf[c, 2:5, 0:128] = sum_buf[4, 0:3]
    image_dot(2)
    image_dot(3)
    every_dot = over_col(dot_buf, 1)
    pairs_sent = remote(sib_buf, sib_buf, pair_sent.at[0], pair_sems.at[0], sibling)
    texts_sent = remote(txt.at[pl.ds(0, 576), :], txt.at[pl.ds(0, 576), :], sib_sent.at[0], sib_sems.at[0], sibling)
    for copy in (pairs_sent, texts_sent):
        copy.wait_send()
    for ring in first + second + [gz] + back_1 + back_2 + [sz]:
        ring.finish()
    dots = every_dot()
    scale_t = scale_buf[1:2, :]
    gt_ref[...] = scale_t * (tg[...] - tx_ref[...] * scale_t * dots[1:2, :])
    for g in range(4):
        cols = slice(g * 128, g * 128 + 128)
        scale = scale_buf[0:1, cols]
        gi_ref[:, cols] = scale * (image_sum(g) - im_ref[:, cols] * scale * dots[0:1, cols])
    means = jnp.sum(dots[:, 0:128], axis=1, keepdims=True) * (1.0 / float(16384 * 16384))
    mean_ref[...] = jnp.broadcast_to(means, (8, 128))
    mean_ref[3:4, :] = mean_ref[3:4, :] * temper[:, 0:128]

    finish_all(started)


def hand_over(mean_ref, gi_in, gt_in, loss_ref, gi_out, gt_out, glt_ref, gb_ref, sems):
    copies = [
        pltpu.make_async_copy(gi_in, gi_out, sems.at[0]),
        pltpu.make_async_copy(gt_in, gt_out, sems.at[1]),
    ]
    for copy in copies:
        copy.start()
    loss_ref[0] = mean_ref[2, 0]
    glt_ref[0] = mean_ref[3, 0]
    gb_ref[0] = mean_ref[4, 0]
    for copy in copies:
        copy.wait()


def per_device(images, texts, log_temp, bias, cid=0, name="contrastive"):
    vmem = pl.BlockSpec(memory_space=pltpu.VMEM)
    smem = pl.BlockSpec(memory_space=pltpu.SMEM)
    anywhere = pl.BlockSpec(memory_space=pl.ANY)
    one = jax.ShapeDtypeStruct((1,), F32)
    grad = jax.ShapeDtypeStruct((SHARE, PAIRS), F32)
    scratch = [
        pltpu.VMEM((8, 8, PAIRS), F32),
        pltpu.VMEM((8, 8, PAIRS), F32),
        pltpu.VMEM((8, PAIRS), F32),
        pltpu.VMEM((SHARE, PAIRS), BF16),
        pltpu.VMEM((2, 4, 2 * SHARE, 512), BF16),
        pltpu.VMEM((FEATURES, 1024), BF16),
        pltpu.VMEM((1024, FEATURES), BF16),
        pltpu.VMEM((1024, 1024), BF16),
        pltpu.VMEM((4, 4, 4, SHARE, 128), F32),
        pltpu.VMEM((8, 1168, 128), F32),
        pltpu.VMEM((8, 576, 128), F32),
        pltpu.VMEM((4, 3, 4, SHARE, 128), F32),
        pltpu.VMEM((4, 3, SHARE, 128), F32),
        pltpu.VMEM((14, 296, 128), F32),
        pltpu.VMEM((3, 8, 128), F32),
        pltpu.VMEM((5, 8, 128), F32),
        pltpu.VMEM((SHARE, PAIRS), F32),
        DMA((2, 2)),
        DMA((2, 2)),
        DMA((1,)),
        DMA((8,)),
        DMA((1,)),
        DMA((4,)),
        DMA((2, 2)),
        DMA((4,)),
        DMA((4, 3)),
        DMA((1,)),
        DMA((14,)),
        DMA((4,)),
        DMA((4, 3)),
        DMA((2, 4)),
        DMA((1,)),
        DMA((14,)),
        DMA((2, 2, 1)),
    ]
    row = lax.broadcasted_iota(jnp.int32, (8, 256), 0)
    knobs = jnp.where(row == 0, log_temp, bias)
    means = jax.ShapeDtypeStruct((8, 128), F32)
    parts = pl.pallas_call(
        kernel,
        out_shape=(means, grad, grad),
        in_specs=[vmem] * 3,
        out_specs=[vmem] * 3,
        scratch_shapes=scratch,
        compiler_params=pltpu.CompilerParams(
            collective_id=cid, has_side_effects=True, vmem_limit_bytes=38 * 2**20
        ),
        name=name,
    )(images, texts, knobs)
    return pl.pallas_call(
        hand_over,
        out_shape=(one, grad, grad, one, one),
        in_specs=[vmem] * 3,
        out_specs=[smem, anywhere, anywhere, smem, smem],
        scratch_shapes=[DMA((2,))],
        compiler_params=pltpu.CompilerParams(vmem_limit_bytes=4 * 2**20),
        name="hand_over",
    )(*parts)


def solution(mesh):
    in_specs = (P("col", "blk"), P("col", "blk"), P(), P())
    out_specs = (P(), P("col", "blk"), P("col", "blk"), P(), P())
    return jax.shard_map(
        per_device, mesh=mesh, in_specs=in_specs, out_specs=out_specs, check_vma=False
    )
```
